32 devices in a mesh: expert: 4 (over y, core), fsdp: 8 (over z, x).
Axes of the slice: x: 2, y: 2, z: 4, core: 2. Of those that a mesh axis runs over, the one named last changes fastest.
Arguments:
- tokens: bfloat16 [4096, 2048], P(('expert', 'fsdp')), may hold values from -6 to 6
- expert_ids: int32 [4096, 4], P(('expert', 'fsdp')), may hold values from 0 to 7, all different within a row; in each aligned block of 128 rows (0 to 127, 128 to 255, ...) at most 128 rows name the same one
- w_query: float32 [2048, 2048], P(('expert', 'fsdp')), may hold values from -0.125 to 0.125
- b_query: float32 [2048], P(('expert', 'fsdp')), may hold values from -3 to 3
- w_key: float32 [2048, 2048], P(('expert', 'fsdp')), may hold values from -0.125 to 0.125
- b_key: float32 [2048], P(('expert', 'fsdp')), may hold values from -3 to 3
- w_value: float32 [2048, 2048], P(('expert', 'fsdp')), may hold values from -0.125 to 0.125
- b_value: float32 [2048], P(('expert', 'fsdp')), may hold values from -3 to 3
- w_output: float32 [2048, 2048], P(('expert', 'fsdp')), may hold values from -1 to 1
- attn_gain: float32 [2048], P(('expert', 'fsdp')), may hold values from 0.5 to 1.5
- ffn_gain: float32 [2048], P(('expert', 'fsdp')), may hold values from 0.5 to 1.5
- w_router: float32 [2048, 8], P(('expert', 'fsdp')), may hold values from -0.0625 to 0.0625
- shared_gate: float32 [2048], P(('expert', 'fsdp')), may hold values from -0.125 to 0.125
- shared_wgate: float32 [2048, 5632], P(('expert', 'fsdp')), may hold values from -0.125 to 0.125
- shared_wup: float32 [2048, 5632], P(('expert', 'fsdp')), may hold values from -0.125 to 0.125
- shared_wdown: float32 [5632, 2048], P(('expert', 'fsdp')), may hold values from -0.15625 to 0.15625
- expert_wgate: float32 [8, 2048, 1408], P('expert', 'fsdp'), may hold values from -0.125 to 0.125
- expert_wup: float32 [8, 2048, 1408], P('expert', 'fsdp'), may hold values from -0.125 to 0.125
- expert_wdown: float32 [8, 1408, 2048], P('expert', None, 'fsdp'), may hold values from -0.4375 to 0.4375
- cotangent: bfloat16 [4096, 2048], P(('expert', 'fsdp')), may hold values from -6 to 6
Outputs:
- output: bfloat16 [4096, 2048], P(('expert', 'fsdp'))
- token_grad: bfloat16 [4096, 2048], P(('expert', 'fsdp'))
- grad_w_query: float32 [2048, 2048], P(('expert', 'fsdp'))
- grad_b_query: float32 [2048], P(('expert', 'fsdp'))
- grad_w_key: float32 [2048, 2048], P(('expert', 'fsdp'))
- grad_b_key: float32 [2048], P(('expert', 'fsdp'))
- grad_w_value: float32 [2048, 2048], P(('expert', 'fsdp'))
- grad_b_value: float32 [2048], P(('expert', 'fsdp'))
- grad_w_output: float32 [2048, 2048], P(('expert', 'fsdp'))
- grad_attn_gain: float32 [2048], P(('expert', 'fsdp'))
- grad_ffn_gain: float32 [2048], P(('expert', 'fsdp'))
- grad_w_router: float32 [2048, 8], P(('expert', 'fsdp'))
- grad_shared_gate: float32 [2048], P(('expert', 'fsdp'))
- grad_shared_wgate: float32 [2048, 5632], P(('expert', 'fsdp'))
- grad_shared_wup: float32 [2048, 5632], P(('expert', 'fsdp'))
- grad_shared_wdown: float32 [5632, 2048], P(('expert', 'fsdp'))
- grad_expert_wgate: float32 [8, 2048, 1408], P('expert', 'fsdp')
- grad_expert_wup: float32 [8, 2048, 1408], P('expert', 'fsdp')
- grad_expert_wdown: float32 [8, 1408, 2048], P('expert', None, 'fsdp')
The draws below stay inside these ranges and needn't reach their ends.
Inputs may be any that keep to these rules, and one draw needn't show every extreme that they name: `expert_ids`: each row names 4 different experts. Among the 128 rows of one device no expert is named more than 128 times, and in every draw some expert is named exactly 128 times by the rows of some device.
All inputs are finite; a program needn't handle non-finite values.
Results may differ from the reference program's by a relative error of at most 0.02.
The reference program's roundings to bfloat16 on the way count: a program that leaves them out, or rounds other values in their place, can miss the bound.
Values may be sent and summed in bfloat16 or wider, within the bound.
No kernel may reach another device: no remote copies, remote signals or barrier semaphores. Data moves between devices by JAX's collectives and lax.ppermute only.
A program may use at most 512 MiB of HBM per device.

```python
import math
import jax
import jax.numpy as jnp
import numpy as np
from jax import lax

WIDTH_SIZE = 2048
HEADS = 16
HEAD_DIM = 128
FE = 1408
FS = 5632
TOP = 4
TOK_DEV = 128
EXPERTS = 8
SEQ = 1024
TOKENS = 4096
MOST = 128
N_EXPERT = 4


def with_spikes(array, own_key, source, target, parts, factor):
    owner, partner = [(jnp.arange(array.shape[axis_at]) // (array.shape[axis_at] // parts)).reshape([-1 if axis == axis_at else 1 for axis in range(array.ndim)]) for axis_at in (source, target)]
    chosen = jax.random.permutation(own_key, parts)[partner]
    strong = (owner == chosen) | (owner == (partner + parts // 2) % parts)
    return jnp.where(strong, factor * array, array)


def levels(key, shape, split, smallest, top_value):
    def one(dim, shards_of):
        draws = jax.random.uniform(jax.random.fold_in(jax.random.fold_in(key, 6), dim), (shards_of,), jnp.float32, smallest / len(split), top_value / len(split))
        return jnp.repeat(jnp.exp(draws), shape[dim] // shards_of).reshape((-1,) + (1,) * (len(shape) - dim - 1))

    level = one(*split[0])
    for cut in split[1:]:
        level = level * one(*cut)
    return level


def assign_block(stream_key, own, number, rows, number_of, top, limit, skew):
    order = jax.random.permutation(stream_key, number_of)
    packed, ordinary = shares(number_of, rows * top, limit, skew, True), shares(number_of, rows * top, limit, skew, False)
    places = jnp.arange(number_of)

    def named(lengths, offset_by):
        used = int((lengths > 0).sum())
        fixed = max(1, used // 4)
        moved = fixed + (places - fixed + offset_by * (used - fixed)) % max(1, number_of - fixed)
        return jnp.zeros((number_of,), jnp.int32).at[order[jnp.where(places < fixed, places, moved)]].set(jnp.asarray(lengths, jnp.int32))

    lengths = jnp.where(number % 4 == 0, named(packed, number // 4), named(ordinary, number - number // 4 - 1))
    mixed = jax.random.permutation(jax.random.fold_in(own, 3), number_of)
    donor, receiver = mixed[0:number_of // 2 * 2:2], mixed[1:number_of // 2 * 2:2]
    room = jnp.minimum(lengths[donor] - 1, limit - lengths[receiver]) // 2
    room = jnp.where((donor == order[0]) | (receiver == order[0]) | (lengths[receiver] == 0), 0, jnp.maximum(room, 0))
    moved = jax.random.randint(jax.random.fold_in(own, 4), (number_of // 2,), 0, 1 << 20) % (room + 1)
    lengths = lengths.at[donor].add(-moved).at[receiver].add(moved)
    members = jnp.searchsorted(jnp.cumsum(lengths), jnp.arange(rows * top), side="right").astype(jnp.int32)
    listing = members.reshape(top, rows).T
    listing = listing[jax.random.permutation(jax.random.fold_in(own, 1), rows)]
    offset_by = jax.random.randint(jax.random.fold_in(own, 2), (rows, 1), 0, top)
    return jnp.take_along_axis(listing, (jnp.arange(top)[None, :] + offset_by) % top, axis=1)


def shares(number_of, total, reach, skew, full):
    loads = [(1 << 20) // math.isqrt(rank ** skew) + 1 for rank in range(1, number_of + 1)]
    largest = reach if full else min(reach, max(-(-total // number_of), total * loads[0] // sum(loads)))
    least = 1 if total - largest >= number_of - 1 else 0
    counts, spare = [largest] + [least] * (number_of - 1), total - largest - least * (number_of - 1)
    while spare > 0:
        free = [i for i in range(1, number_of) if counts[i] < largest] or [i for i in range(1, number_of) if counts[i] < reach]
        mass, left = sum([loads[i] for i in free]), spare
        for i in free:
            extra = min(reach - counts[i], max(1, left * loads[i] // mass), spare)
            counts[i] = counts[i] + extra
            spare = spare - extra
    return np.array(counts)


def normal_values(rng, dims, spread, limit, split=(), kind=jnp.bfloat16):
    values = jax.random.normal(rng, dims, jnp.float32) * spread
    if len(split) > 0:
        values = levels(rng, dims, split, -0.22, 0.18) * values
    return jnp.clip(values, min=-limit, max=limit).astype(kind)


def heavy_noise(key, shape, scale, reach, cuts, heavy, held_as=jnp.bfloat16):
    values = scale * jax.random.normal(key, shape, jnp.float32)
    if cuts:
        values = values * levels(key, shape, cuts, -0.22, 0.18)
    return jnp.clip(with_spikes(values, jax.random.fold_in(key, 3), *heavy), -reach, reach).astype(held_as)


def setup_inputs(seed: int = 0) -> dict:
    splits = jax.random.split(jax.random.key(seed), 21)
    tokens = heavy_noise(splits[0], (TOKENS, WIDTH_SIZE), 1.0, 6.0, ((0, 32),), (0, 1, 32, 2.75))
    expert_ids_keys = jax.random.split(jax.random.fold_in(splits[1], 1), TOKENS // TOK_DEV)
    expert_ids_turns = jax.random.permutation(jax.random.fold_in(splits[1], 3), TOKENS // TOK_DEV)
    expert_ids = jax.vmap(lambda own, number: assign_block(jax.random.fold_in(splits[1], 2), own, number, TOK_DEV, EXPERTS, TOP, MOST, 2))(expert_ids_keys, expert_ids_turns).reshape((TOKENS, TOP))
    w_query = normal_values(splits[2], (WIDTH_SIZE, WIDTH_SIZE), WIDTH_SIZE ** -0.5, 0.125, ((0, 32),), jnp.float32)
    b_query = normal_values(splits[3], (WIDTH_SIZE,), 0.5, 3.0, ((0, 32),), jnp.float32)
    w_key = normal_values(splits[4], (WIDTH_SIZE, WIDTH_SIZE), WIDTH_SIZE ** -0.5, 0.125, ((0, 32),), jnp.float32)
    b_key = normal_values(splits[5], (WIDTH_SIZE,), 0.5, 3.0, ((0, 32),), jnp.float32)
    w_value = normal_values(splits[6], (WIDTH_SIZE, WIDTH_SIZE), WIDTH_SIZE ** -0.5, 0.125, ((0, 32),), jnp.float32)
    b_value = normal_values(splits[7], (WIDTH_SIZE,), 0.5, 3.0, ((0, 32),), jnp.float32)
    w_output = normal_values(splits[8], (WIDTH_SIZE, WIDTH_SIZE), (WIDTH_SIZE // 64) ** -0.5, 1.0, ((0, 32),), jnp.float32)
    attn_gain = jnp.clip(1.0 + 0.1 * jax.random.normal(splits[9], (WIDTH_SIZE,), jnp.float32), 0.5, 1.5)
    ffn_gain = jnp.clip(1.0 + 0.1 * jax.random.normal(splits[10], (WIDTH_SIZE,), jnp.float32), 0.5, 1.5)
    w_router = normal_values(splits[11], (WIDTH_SIZE, EXPERTS), (4 * WIDTH_SIZE) ** -0.5, 0.0625, ((0, 32),), jnp.float32)
    shared_gate = normal_values(splits[12], (WIDTH_SIZE,), WIDTH_SIZE ** -0.5, 0.125, ((0, 32),), jnp.float32)
    shared_wgate = normal_values(splits[13], (WIDTH_SIZE, FS), WIDTH_SIZE ** -0.5, 0.125, ((0, 32),), jnp.float32)
    shared_wup = normal_values(splits[14], (WIDTH_SIZE, FS), WIDTH_SIZE ** -0.5, 0.125, ((0, 32),), jnp.float32)
    shared_wdown = normal_values(splits[15], (FS, WIDTH_SIZE), (FS // 4) ** -0.5, 0.15625, ((0, 32),), jnp.float32)
    expert_wgate = normal_values(splits[16], (EXPERTS, WIDTH_SIZE, FE), WIDTH_SIZE ** -0.5, 0.125, ((0, 4), (1, 8)), jnp.float32)
    expert_wup = normal_values(splits[17], (EXPERTS, WIDTH_SIZE, FE), WIDTH_SIZE ** -0.5, 0.125, ((0, 4), (1, 8)), jnp.float32)
    expert_wdown = normal_values(splits[18], (EXPERTS, FE, WIDTH_SIZE), (FE // (EXPERTS * EXPERTS // 8)) ** -0.5, 0.4375, ((0, 4), (2, 8)), jnp.float32)
    cotangent = normal_values(splits[19], (TOKENS, WIDTH_SIZE), 1.0, 6.0, ((0, 32),))
    return {"tokens": tokens, "expert_ids": expert_ids, "w_query": w_query, "b_query": b_query, "w_key": w_key, "b_key": b_key, "w_value": w_value, "b_value": b_value, "w_output": w_output, "attn_gain": attn_gain, "ffn_gain": ffn_gain, "w_router": w_router, "shared_gate": shared_gate, "shared_wgate": shared_wgate, "shared_wup": shared_wup, "shared_wdown": shared_wdown, "expert_wgate": expert_wgate, "expert_wup": expert_wup, "expert_wdown": expert_wdown, "cotangent": cotangent}


norm_eps = 1e-06
rope_base = 1000000.0
highest = lax.Precision.HIGHEST

@jax.custom_vjp
def low(v):
    return lax.optimization_barrier(v.astype(jnp.bfloat16)).astype(jnp.float32)

@jax.custom_vjp
def low_back(v):
    return v

def low_keep(v):
    return (low(v), None)

def low_pass(kept, grad):
    return (grad,)

def back_keep(v):
    return (v, None)

def back_low(kept, grad):
    return (low(grad),)
low.defvjp(low_keep, low_pass)
low_back.defvjp(back_keep, back_low)

def matmul(left_side, right_side):
    return jnp.dot(left_side, right_side, precision=highest)

def rms_norm(hidden, gain_vec):
    factor = lax.rsqrt(lax.optimization_barrier(jnp.mean(hidden * hidden, axis=-1, keepdims=True)) + norm_eps)
    return hidden * factor * gain_vec

def rope_tables(length):
    half_dim = HEAD_DIM // 2
    places = jnp.arange(length, dtype=jnp.int32).astype(jnp.float32)
    frequency = rope_base ** (-(jnp.arange(half_dim, dtype=jnp.int32).astype(jnp.float32) * 2.0 / HEAD_DIM))
    angles = places[:, None] * frequency[None, :]
    return (jnp.cos(angles)[:, None, :], jnp.sin(angles)[:, None, :])

def rotate(head_rows, cosine_table, sine_table):
    half_dim = head_rows.shape[-1] // 2
    first_half = head_rows[..., :half_dim]
    second_half = head_rows[..., half_dim:]
    return jnp.concatenate([first_half * cosine_table - second_half * sine_table, second_half * cosine_table + first_half * sine_table], axis=-1)

def attend(block):
    query_rows, key_rows, value_rows = block
    scores = low_back(jnp.einsum('qhd,khd->hqk', query_rows, key_rows, precision=highest))
    places = jnp.arange(query_rows.shape[0], dtype=jnp.int32)
    causal = places[:, None] >= places[None, :]
    scores = jnp.where(causal[None], scores, -1e+30)
    attn_probs = jax.nn.softmax(scores, axis=-1)
    return jnp.einsum('hqk,khd->qhd', low(attn_probs), value_rows, precision=highest)

def forward(selected, tokens, w_query, b_query, w_key, b_key, w_value, b_value, w_output, attn_gain, ffn_gain, w_router, shared_gate, shared_wgate, shared_wup, shared_wdown, expert_wgate, expert_wup, expert_wdown):
    parameters = jax.tree.map(low, (w_query, b_query, w_key, b_key, w_value, b_value, w_output, attn_gain, ffn_gain, w_router, shared_gate, shared_wgate, shared_wup, shared_wdown, expert_wgate, expert_wup, expert_wdown))
    query_weight, query_bias, key_weight, key_bias, value_weight, value_bias, output_weight, attention_scale, feedforward_scale, router_weight, gate_vector, shared_gate_weight, shared_up_weight, shared_down_weight, expert_gate_weight, expert_up_weight, expert_down_weight = parameters
    count_of_tokens = tokens.shape[0]
    score_scale = HEAD_DIM ** (-0.5)

    def heads_of(flat_rows):
        return flat_rows.reshape(N_EXPERT, SEQ, HEADS, HEAD_DIM)
    normed = low(rms_norm(tokens, attention_scale))
    cosine_table, sine_table = rope_tables(SEQ)
    query_lin = low_back(matmul(normed, query_weight) + query_bias)
    query_rows = low(rotate(heads_of(query_lin), cosine_table, sine_table) * score_scale)
    key_lin = low_back(matmul(normed, key_weight) + key_bias)
    key_rows = low(rotate(heads_of(key_lin), cosine_table, sine_table))
    value_rows = low(low_back(matmul(normed, value_weight) + value_bias))
    mixed_heads = lax.map(jax.checkpoint(attend), (query_rows, key_rows, heads_of(value_rows)))
    mixed_heads = low(low_back(mixed_heads.reshape(count_of_tokens, WIDTH_SIZE)))
    attn_out = low_back(matmul(mixed_heads, output_weight))
    hidden = tokens + attn_out
    ffn_input = low(rms_norm(hidden, feedforward_scale))
    route_probs = jax.nn.softmax(matmul(ffn_input, router_weight), axis=-1)
    gate_weights_picked = route_probs * selected
    shared_weight = jax.nn.sigmoid(matmul(ffn_input, gate_vector))
    gate_lin = low_back(matmul(ffn_input, shared_gate_weight))
    up_lin = low_back(matmul(ffn_input, shared_up_weight))
    shared_mid = low(jax.nn.silu(gate_lin) * up_lin)
    shared_out = low_back(matmul(shared_mid, shared_down_weight))

    def expert_update(running, pieces):
        wgate_one, wup_one, wdown_one, gate_column = pieces
        routed = low_back(ffn_input)
        gate_part = low_back(matmul(routed, wgate_one))
        up_part = low_back(matmul(routed, wup_one))
        middle = low(jax.nn.silu(gate_part) * up_part)
        result = low(low_back(matmul(middle, wdown_one)))
        return (running + gate_column[:, None] * result, None)
    expert_output_sum, unused_value = lax.scan(jax.checkpoint(expert_update), jnp.zeros((count_of_tokens, WIDTH_SIZE), jnp.float32), (expert_gate_weight, expert_up_weight, expert_down_weight, gate_weights_picked.T))
    return hidden + expert_output_sum + shared_weight[:, None] * shared_out

def reference(tokens, expert_ids, w_query, b_query, w_key, b_key, w_value, b_value, w_output, attn_gain, ffn_gain, w_router, shared_gate, shared_wgate, shared_wup, shared_wdown, expert_wgate, expert_wup, expert_wdown, cotangent):
    selected = lax.optimization_barrier(jnp.sum(jax.nn.one_hot(expert_ids, EXPERTS, dtype=jnp.float32), axis=1))
    floats = jax.tree.map(lambda element: element.astype(jnp.float32), (tokens, w_query, b_query, w_key, b_key, w_value, b_value, w_output, attn_gain, ffn_gain, w_router, shared_gate, shared_wgate, shared_wup, shared_wdown, expert_wgate, expert_wup, expert_wdown))
    output, pull_back = jax.vjp(lambda *inputs: forward(selected, *inputs), *floats)
    gradients = pull_back(cotangent.astype(jnp.float32))
    return (output.astype(jnp.bfloat16), gradients[0].astype(jnp.bfloat16), gradients[1], gradients[2], gradients[3], gradients[4], gradients[5], gradients[6], gradients[7], gradients[8], gradients[9], gradients[10], gradients[11], gradients[12], gradients[13], gradients[14], gradients[15], gradients[16], gradients[17])
```

```python
import jax
import jax.numpy as jnp
from jax import lax
from jax.sharding import PartitionSpec as P

HEADS = 16
HEAD_DIM = 128
HALF = HEAD_DIM // 2

E = "expert"
F = "fsdp"
EF = (E, F)

norm_eps = 1e-06
rope_base = 1000000.0
highest = lax.Precision.HIGHEST
bf16 = jnp.bfloat16
f32 = jnp.float32


def dot(left, right, left_dim, right_dim, precision=None):
    return lax.dot_general(
        left,
        right,
        (((left_dim,), (right_dim,)), ((), ())),
        precision=precision,
        preferred_element_type=f32,
    )


def product(left, right):
    return dot(left, right, 1, 0)


def product_t(left, right):
    return dot(left, right, 1, 1)


def contract(left, right):
    return dot(left, right, 0, 0)


def inverse_rms(rows):
    return lax.rsqrt(jnp.mean(rows * rows, axis=-1, keepdims=True) + norm_eps)


def norm_back(rows, gain, grad):
    factor = inverse_rms(rows)
    scaled = grad * gain
    along = jnp.mean(rows * scaled, axis=-1, keepdims=True)
    return factor * scaled - rows * (factor * factor * factor * along), rows * factor


def rope_tables(places):
    places = places.astype(f32)
    frequency = rope_base ** (-(jnp.arange(HALF, dtype=jnp.int32).astype(f32) * 2.0 / HEAD_DIM))
    angles = places[:, None] * frequency[None, :]
    cosine, sine = jnp.cos(angles), jnp.sin(angles)
    return jnp.concatenate([cosine, cosine], axis=1), jnp.concatenate([-sine, sine], axis=1)


def swap(head):
    return jnp.concatenate([head[:, HALF:], head[:, :HALF]], axis=1)


def ring_order(size):
    levels = 4 if size % 4 == 0 else size
    across = size // levels
    return [
        level * across + at
        for at in range(across)
        for level in (range(levels) if at % 2 == 0 else reversed(range(levels)))
    ]


def ring_shift(size, by):
    order = ring_order(size)
    return [(order[i], order[(i + by) % size]) for i in range(size)]


def ring_neighbour(by):
    size = lax.axis_size(F)
    order = ring_order(size)
    places = [order.index(f) for f in range(size)]
    at = jnp.array(places, jnp.int32)[lax.axis_index(F)]
    return jnp.array(order, jnp.int32)[(at + by) % size]


def ring_gather(shard, ties=None):
    ties = ties or {}
    size = lax.axis_size(F)
    right, left = ring_shift(size, 1), ring_shift(size, -1)
    rows = shard.shape[0]
    cut = rows // 2
    whole = jnp.zeros((size * rows,) + shard.shape[1:], shard.dtype)

    def put(whole, block, by, first=0):
        return lax.dynamic_update_slice_in_dim(
            whole, block, ring_neighbour(by) * rows + first, 0
        )

    up = down = shard
    whole = put(whole, shard, 0)
    for step in range(1, size // 2):
        up, down = tied(up, down, ties.get(step))
        up, down = lax.ppermute(up, F, right), lax.ppermute(down, F, left)
        whole = put(put(whole, up, -step), down, step)
    up, down = tied(up, down, ties.get(size // 2))
    up, down = lax.ppermute(up[:cut], F, right), lax.ppermute(down[cut:], F, left)
    return put(put(whole, up, size // 2), down, size // 2, cut)


def ring_scatter(terms, ties=None):
    ties = ties or {}
    size = lax.axis_size(F)
    right, left = ring_shift(size, 1), ring_shift(size, -1)
    half = size // 2
    rows = terms.shape[0] // size
    cut = rows // 2

    def block(by):
        return lax.dynamic_slice_in_dim(terms, ring_neighbour(by) * rows, rows, 0)

    opposite = block(half).astype(bf16)
    up, down = opposite[:cut], opposite[cut:]
    for step in range(half - 1, 0, -1):
        up, down = lax.ppermute(up, F, right), lax.ppermute(down, F, left)
        plus, minus = block(step).astype(f32), block(-step).astype(f32)
        if step == half - 1:
            plus = jnp.concatenate([plus[:cut] + up.astype(f32), plus[cut:]])
            minus = jnp.concatenate([minus[:cut], minus[cut:] + down.astype(f32)])
        else:
            plus, minus = plus + up.astype(f32), minus + down.astype(f32)
        up, down = tied(plus.astype(bf16), minus.astype(bf16), ties.get(step))
    up, down = lax.ppermute(up, F, right), lax.ppermute(down, F, left)
    up, down = tied(up, down, ties.get(0))
    return block(0).astype(f32) + up.astype(f32) + down.astype(f32)


def tied(up, down, tie):
    if tie is None:
        return up, down
    return lax.optimization_barrier((up, down, tie))[:2]


def pick(blocks, index):
    return lax.dynamic_index_in_dim(blocks, index, 0, keepdims=False)


def swap_blocks(blocks, axis):
    return lax.all_to_all(blocks, axis, split_axis=0, concat_axis=0, tiled=True)


def sibling(value):
    return lax.ppermute(value, E, [(e, e ^ 1) for e in range(lax.axis_size(E))])


def along_y(value, by):
    size = lax.axis_size(E)
    return lax.ppermute(value, E, [(e, (e + 2 * by) % size) for e in range(size)])


def gather_e(block):
    size, at = lax.axis_size(E), lax.axis_index(E)
    levels, rows = size // 2, block.shape[0]
    whole = jnp.zeros((size * rows,) + block.shape[1:], block.dtype)
    for by in range(levels):
        came = along_y(block, by) if by else block
        source = 2 * ((at // 2 - by) % levels) + at % 2
        whole = lax.dynamic_update_slice_in_dim(whole, came, source * rows, 0)
        whole = lax.dynamic_update_slice_in_dim(whole, sibling(came), (source ^ 1) * rows, 0)
    return whole


def reduce_e(blocks):
    size, at = lax.axis_size(E), lax.axis_index(E)
    levels, core = size // 2, at % 2
    blocks = blocks.reshape((levels, 2) + blocks.shape[1:])
    mine = lax.dynamic_index_in_dim(blocks, core, 1, keepdims=False)
    theirs = lax.dynamic_index_in_dim(blocks, 1 - core, 1, keepdims=False)
    mine = mine + sibling(theirs.astype(bf16)).astype(f32)
    total = pick(mine, at // 2)
    for by in range(1, levels):
        total = total + along_y(pick(mine, (at // 2 + by) % levels).astype(bf16), by).astype(f32)
    return total


def after(value, *others):
    return lax.optimization_barrier((value,) + others)[0]


def shards(
    tokens,
    expert_ids,
    w_query,
    b_query,
    w_key,
    b_key,
    w_value,
    b_value,
    w_output,
    attn_gain,
    ffn_gain,
    w_router,
    shared_gate,
    shared_wgate,
    shared_wup,
    shared_wdown,
    expert_wgate,
    expert_wup,
    expert_wdown,
    cotangent,
):
    n_e, n_f = lax.axis_size(E), lax.axis_size(F)
    devices = n_e * n_f
    at_e, at_f = lax.axis_index(E), lax.axis_index(F)
    rows, width = tokens.shape
    seq = rows * n_f
    slab = width // n_f
    part = width // devices
    heads = HEADS // n_f
    experts, top = w_router.shape[1], expert_ids.shape[1]
    own = experts // n_e
    per_expert = expert_wgate.shape[2] // n_f
    per_shared = shared_wdown.shape[0]
    hidden_own = own * per_expert + per_shared
    score_scale = HEAD_DIM ** (-0.5)

    small = jnp.concatenate(
        [
            jnp.stack([b_query, b_key, b_value, attn_gain, ffn_gain, shared_gate]).astype(bf16),
            w_router.T.astype(bf16),
            expert_ids.T.astype(bf16).reshape(-1, part),
        ]
    )
    small_all = swap_blocks(jnp.broadcast_to(small, (devices,) + small.shape), EF)
    vectors = small_all[:, : 6 + experts].transpose(1, 0, 2).reshape(6 + experts, width)
    ids_all = small_all[:, 6 + experts :].reshape(n_e, n_f, top, rows)

    def ids_of(e):
        return pick(ids_all, e).transpose(0, 2, 1).reshape(seq, top)

    biases = lax.dynamic_slice_in_dim(vectors[:3], at_f * slab, slab, 1).astype(f32)
    gain_one = vectors[3].astype(f32)
    gain_two = vectors[4].astype(f32)
    route_rows = vectors[5:]

    w_out = lax.all_gather(w_output.astype(bf16), EF, axis=0, tiled=True)
    qkv_own = jnp.stack([w_query, w_key, w_value]).astype(bf16).reshape(3, part, n_f, slab)
    qkv_own = swap_blocks(qkv_own.transpose(2, 1, 0, 3).reshape(n_f, part, 3 * slab), F)
    w_qkv = gather_e(qkv_own.reshape(n_f * part, 3 * slab))

    def by_hidden(expert_weight, shared_weight):
        routed = expert_weight.astype(bf16).transpose(0, 2, 1).reshape(own, n_f, per_expert, slab)
        routed = routed.transpose(1, 0, 2, 3).reshape(n_f, own * per_expert, slab)
        shared = shared_weight.T.reshape(n_f, per_shared, slab)
        return jnp.concatenate([routed, shared], axis=1)

    shared_two = jnp.stack([shared_wgate, shared_wup]).astype(bf16)
    shared_two = shared_two.reshape(2, part, n_e, n_f * per_shared).transpose(2, 0, 1, 3)
    shared_two = swap_blocks(shared_two.reshape(n_e, 2 * part, n_f * per_shared), E)
    shared_two = shared_two.reshape(n_e, 2, part, n_f * per_shared).transpose(1, 0, 2, 3)
    shared_two = shared_two.reshape(2, n_e * part, n_f * per_shared)
    gate_blocks = by_hidden(expert_wgate, shared_two[0])
    up_blocks = by_hidden(expert_wup, shared_two[1])
    routed_down = expert_wdown.astype(bf16).reshape(own, n_f, per_expert, slab)
    routed_down = routed_down.transpose(1, 0, 2, 3).reshape(n_f, own * per_expert, slab)

    def full_width(blocks):
        return blocks.transpose(1, 0, 2).reshape(blocks.shape[1], width)

    def gate_like(mine):
        routed = full_width(mine[:, : own * per_expert])
        shared = mine[:, own * per_expert :].reshape(n_f, per_shared, n_e, part)
        shared = shared.transpose(1, 2, 0, 3).reshape(per_shared, width)
        return jnp.concatenate([routed, shared])

    def both_levels(mine):
        return jnp.concatenate([mine] + [along_y(mine, by) for by in range(1, levels)])

    levels = n_e // 2
    x_all = ring_gather(tokens, {n_f // 2: (qkv_own, gate_blocks, up_blocks, routed_down)})
    gate_mine = swap_blocks(after(gate_blocks, x_all), F)
    up_mine = swap_blocks(after(up_blocks, x_all), F)

    blocks = own + 1
    column = jnp.arange(levels * hidden_own, dtype=jnp.int32)
    level_of = (at_e // 2 - column // hidden_own) % levels
    block_of = (2 * level_of + at_e % 2) * blocks + jnp.minimum(
        (column % hidden_own) // per_expert, own
    )
    spread = (jnp.arange(n_e * blocks, dtype=jnp.int32)[:, None] == block_of[None, :]).astype(f32)

    x_wide = x_all.astype(f32)
    x_hat = x_wide * inverse_rms(x_wide)
    normed = (x_hat * gain_one).astype(bf16)
    places = jnp.arange(seq, dtype=jnp.int32)
    cosine, sine = rope_tables(places)
    lin = product(normed, w_qkv)
    causal = places[:, None] >= places[None, :]
    saved, mixed_parts = [], []
    for h in range(heads):
        at = h * HEAD_DIM
        q_lin, k_lin, v_lin = [
            lin[:, i * slab + at : i * slab + at + HEAD_DIM] + biases[i, at : at + HEAD_DIM]
            for i in range(3)
        ]
        q = ((q_lin * cosine + swap(q_lin) * sine) * score_scale).astype(bf16)
        k = (k_lin * cosine + swap(k_lin) * sine).astype(bf16)
        v = v_lin.astype(bf16)
        scores = jnp.where(causal, product_t(q, k), -1e30)
        top_score = jnp.max(scores, axis=-1, keepdims=True)
        log_total = top_score + jnp.log(
            jnp.sum(jnp.exp(scores - top_score), axis=-1, keepdims=True)
        )
        probs = jnp.exp(scores - log_total)
        mixed_parts.append(product(probs.astype(bf16), v).astype(bf16))
        saved.append((q, k, v, probs))
    mixed = jnp.concatenate(mixed_parts, axis=1)
    gate_mine = gate_like(after(gate_mine, mixed))
    w_gate = both_levels(gate_mine)
    mixed_own = swap_blocks(mixed.reshape(n_f, rows, slab), F)
    up_mine = gate_like(after(up_mine, mixed_own))
    mixed_own = mixed_own.transpose(1, 0, 2).reshape(rows, width)
    hidden = tokens.astype(f32) + product(mixed_own, w_out)

    ffn_own = (hidden * inverse_rms(hidden) * gain_two).astype(bf16)
    w_up = both_levels(up_mine)
    g_all = lax.all_gather(after(cotangent, mixed_own), F, axis=0, tiled=True)
    g_both = jnp.concatenate([g_all, sibling(g_all)])
    down_mine = swap_blocks(after(routed_down, mixed_own), F)
    ffn_all = ring_gather(after(ffn_own, up_mine))
    ffn_both = jnp.concatenate([ffn_all, sibling(ffn_all)])
    down_mine = full_width(after(down_mine, ffn_all))
    down_mine = jnp.concatenate([down_mine, shared_wdown.astype(bf16)])
    w_down = both_levels(down_mine)

    named = jnp.arange(experts, dtype=jnp.int32).astype(bf16)
    ids = jnp.concatenate([ids_of(at_e), ids_of(at_e ^ 1)])
    selected = jnp.sum((ids[:, :, None] == named).astype(f32), axis=1)
    logits = product_t(ffn_both, route_rows)
    logit_exp = jnp.exp(logits[:, 1:] - jnp.max(logits[:, 1:], axis=-1, keepdims=True))
    route_probs = logit_exp / jnp.sum(logit_exp, axis=-1, keepdims=True)
    shared_scale = jax.nn.sigmoid(logits[:, :1])
    gates = jnp.concatenate(
        [
            (route_probs * selected).reshape(2 * seq, n_e, own),
            jnp.broadcast_to(shared_scale[:, None, :], (2 * seq, n_e, 1)),
        ],
        axis=2,
    ).reshape(2 * seq, n_e * blocks)
    scale = dot(gates, spread, 1, 0, highest)
    pre_gate = product_t(ffn_both, w_gate)
    pre_up = product_t(ffn_both, w_up)
    sig = jax.nn.sigmoid(pre_gate)
    silu = pre_gate * sig
    slope = sig * (1.0 + pre_gate * (1.0 - sig))
    mid = (silu * pre_up).astype(bf16).astype(f32)
    mid_scaled = (mid * scale).astype(bf16)

    def over_levels(grad):
        total = grad[:hidden_own].astype(f32)
        for by in range(1, levels):
            there = grad[by * hidden_own : (by + 1) * hidden_own]
            total = total + along_y(there, -by).astype(f32)
        return total.astype(bf16)

    d_down_all = contract(mid_scaled, after(g_both, down_mine)).astype(bf16)
    d_down = over_levels(d_down_all)

    mid_grad = product_t(after(g_both, d_down_all), w_down)
    sums = dot(spread, mid * mid_grad, 1, 1, highest)
    scaled = mid_grad * scale
    gate_grad = (scaled * pre_up * slope).astype(bf16)
    up_grad = (scaled * silu).astype(bf16)

    def input_grad(first):
        rows_of = slice(first, first + seq)
        return product(gate_grad[rows_of], w_gate) + product(up_grad[rows_of], w_up)

    from_sibling = sibling(input_grad(seq).astype(bf16))
    moe_sibling = sibling(product(mid_scaled[seq:], w_down).astype(bf16))
    gate_sums = sums[:, :seq] + sibling(sums[:, seq:])
    gate_sums = gate_sums.reshape(n_e * blocks, n_f, rows).transpose(1, 0, 2)
    gate_sums = jnp.sum(swap_blocks(gate_sums, F), axis=0)
    d_gate_all = contract(gate_grad, ffn_both).astype(bf16)
    d_up_all = contract(up_grad, ffn_both).astype(bf16)
    d_gate, d_up = over_levels(d_gate_all), over_levels(d_up_all)
    moe = (product(mid_scaled[:seq], w_down) + moe_sibling.astype(f32)).astype(bf16)
    ffn_grad = ring_scatter(
        (input_grad(0) + from_sibling.astype(f32)).astype(bf16),
        {3: d_gate_all, 2: d_up_all, 1: moe, 0: gate_sums},
    )
    moe = lax.psum_scatter(moe, F, scatter_dimension=0, tiled=True)
    output = (hidden + moe.astype(f32)).astype(bf16)
    gate_sums = gate_sums.T.reshape(rows, n_e, blocks)

    def mine(table):
        return lax.dynamic_slice_in_dim(table, at_f * rows, rows, 0)

    probs_own, shared_own, selected_own = mine(route_probs), mine(shared_scale), mine(selected)
    prob_grad = gate_sums[:, :, :own].reshape(rows, experts) * selected_own
    logit_grad = probs_own * (
        prob_grad - jnp.sum(probs_own * prob_grad, axis=-1, keepdims=True)
    )
    weight_grad = (
        jnp.sum(gate_sums[:, :, own], axis=1, keepdims=True) * shared_own * (1.0 - shared_own)
    )
    route_grad = jnp.concatenate([weight_grad, logit_grad], axis=1)
    d_route = dot(route_grad, ffn_own.astype(f32), 0, 0, highest)
    ffn_grad = ffn_grad + dot(route_grad, route_rows.astype(f32), 1, 0, highest)
    hidden_back, hidden_hat = norm_back(hidden, gain_two, ffn_grad)
    d_gain_two = jnp.sum(ffn_grad * hidden_hat, axis=0)
    hidden_grad = cotangent.astype(f32) + hidden_back

    def by_slab(grad):
        return grad.reshape(grad.shape[0], n_f, slab).transpose(1, 0, 2)

    def gate_slabs(grad):
        routed, shared = grad[: own * per_expert], grad[own * per_expert :]
        shared = shared.reshape(per_shared, n_e, n_f, part).transpose(2, 0, 1, 3)
        shared = shared.reshape(n_f, per_shared, slab)
        return jnp.concatenate([by_slab(routed), shared], axis=1)

    hidden_low = hidden_grad.astype(bf16)
    mixed_grad = product_t(hidden_low, w_out).astype(bf16).reshape(rows, n_f, slab)
    mixed_grad = swap_blocks(mixed_grad.transpose(1, 0, 2), F)
    d_down_back = swap_blocks(by_slab(d_down[: own * per_expert]), F)
    gate_back = swap_blocks(gate_slabs(d_gate), F)
    up_back = swap_blocks(gate_slabs(d_up), F)
    mixed_grad = mixed_grad.reshape(seq, slab)
    hidden_low = lax.all_gather(hidden_low, F, axis=0, tiled=True)
    d_out = contract(mixed, hidden_low)
    lin_grads = [[], [], []]
    for h in range(heads):
        q, k, v, probs = saved[h]
        out_grad = mixed_grad[:, h * HEAD_DIM : (h + 1) * HEAD_DIM]
        p_grad = product_t(out_grad, v)
        delta = jnp.sum(probs * p_grad, axis=-1, keepdims=True)
        s_grad = (probs * (p_grad - delta)).astype(bf16)
        dq = product(s_grad, k) * score_scale
        dk = contract(s_grad, q)
        lin_grads[0].append((dq * cosine - swap(dq) * sine).astype(bf16))
        lin_grads[1].append((dk * cosine - swap(dk) * sine).astype(bf16))
        lin_grads[2].append(contract(probs.astype(bf16), out_grad).astype(bf16))
    lin_grad = jnp.concatenate(lin_grads[0] + lin_grads[1] + lin_grads[2], axis=1)
    normed_part = product_t(lin_grad, w_qkv).astype(bf16)
    d_qkv = contract(normed, lin_grad)
    normed_grad = ring_scatter(normed_part, {3: d_qkv, 1: d_down_back, 0: gate_back})
    d_bias = jnp.sum(lin_grad.astype(f32), axis=0).reshape(3, slab)
    d_gain_one = jnp.sum(d_qkv * w_qkv.astype(f32), axis=1) / gain_one
    token_back, unused = norm_back(tokens.astype(f32), gain_one, normed_grad)
    token_grad = (hidden_grad + token_back).astype(bf16)

    def return_routed(back):
        back = back.reshape(n_f, own, per_expert, slab).transpose(1, 0, 2, 3)
        return back.reshape(own, n_f * per_expert, slab)

    def return_gate(back):
        return return_routed(back[:, : own * per_expert]).transpose(0, 2, 1).astype(f32)

    d_shared_down = d_down[own * per_expert :].astype(f32)
    d_expert_down = return_routed(d_down_back).astype(f32)
    d_expert_gate, d_expert_up = return_gate(gate_back), return_gate(up_back)
    shared_two = jnp.stack([gate_back[:, own * per_expert :], up_back[:, own * per_expert :]])
    shared_two = shared_two.reshape(2, n_f * per_shared, slab).transpose(0, 2, 1)
    shared_two = shared_two.reshape(2, n_e, part, n_f * per_shared).transpose(1, 0, 2, 3)
    shared_two = swap_blocks(shared_two.reshape(n_e, 2 * part, n_f * per_shared), E)
    shared_two = shared_two.reshape(n_e, 2, part, n_f * per_shared).transpose(1, 2, 0, 3)
    shared_two = shared_two.reshape(2, part, devices * per_shared).astype(f32)

    from_heads = [(e * n_f + f, n_e * f + e) for e in range(n_e) for f in range(n_f)]
    d_out = reduce_e(d_out.reshape(n_e, part, width)).astype(bf16)
    d_wout = lax.ppermute(d_out, EF, from_heads).astype(f32)
    d_qkv = reduce_e(d_qkv.reshape(n_e, n_f * part, 3 * slab)).astype(bf16)
    d_qkv = swap_blocks(d_qkv.reshape(n_f, part, 3 * slab), F)
    d_qkv = d_qkv.reshape(n_f, part, 3, slab).transpose(2, 1, 0, 3).reshape(3, part, width)
    d_qkv = d_qkv.astype(f32)

    bias_rows = lax.dynamic_update_slice_in_dim(
        jnp.zeros((3, width), f32), d_bias, at_f * slab, 1
    )
    d_small = jnp.concatenate([bias_rows, d_gain_one[None], d_gain_two[None], d_route])
    d_small = d_small.reshape(6 + experts, n_e, n_f, part).transpose(2, 1, 0, 3)
    d_small = jnp.sum(swap_blocks(d_small, F), axis=0)
    d_small = jnp.sum(swap_blocks(d_small, E), axis=0)

    return (
        output,
        token_grad,
        d_qkv[0],
        d_small[0],
        d_qkv[1],
        d_small[1],
        d_qkv[2],
        d_small[2],
        d_wout,
        d_small[3],
        d_small[4],
        d_small[6:].T,
        d_small[5],
        shared_two[0],
        shared_two[1],
        d_shared_down,
        d_expert_gate,
        d_expert_up,
        d_expert_down,
    )


def solution(mesh):
    matrix, vector = P(EF, None), P(EF)
    wide, tall = P(E, F, None), P(E, None, F)
    in_specs = (matrix, matrix) + (matrix, vector) * 3 + (matrix, vector, vector, matrix, vector)
    in_specs = in_specs + (matrix,) * 3 + (wide, wide, tall, matrix)
    out_specs = (matrix, matrix) + (matrix, vector) * 3 + (matrix, vector, vector, matrix, vector)
    out_specs = out_specs + (matrix,) * 3 + (wide, wide, tall)
    return jax.shard_map(shards, mesh=mesh, in_specs=in_specs, out_specs=out_specs, check_vma=False)
```

```python
import jax
import jax.numpy as jnp
from jax import lax
from jax.sharding import PartitionSpec as P

HEADS = 16
HEAD_DIM = 128
HALF = HEAD_DIM // 2

E = "expert"
F = "fsdp"
EF = (E, F)

norm_eps = 1e-06
rope_base = 1000000.0
highest = lax.Precision.HIGHEST
bf16 = jnp.bfloat16
f32 = jnp.float32


def dot(left, right, left_dim, right_dim, precision=None):
    return lax.dot_general(
        left,
        right,
        (((left_dim,), (right_dim,)), ((), ())),
        precision=precision,
        preferred_element_type=f32,
    )


def product(left, right):
    return dot(left, right, 1, 0)


def product_t(left, right):
    return dot(left, right, 1, 1)


def contract(left, right):
    return dot(left, right, 0, 0)


def inverse_rms(rows):
    return lax.rsqrt(jnp.mean(rows * rows, axis=-1, keepdims=True) + norm_eps)


def norm_back(rows, gain, grad):
    factor = inverse_rms(rows)
    scaled = grad * gain
    along = jnp.mean(rows * scaled, axis=-1, keepdims=True)
    return factor * scaled - rows * (factor * factor * factor * along), rows * factor


def rope_tables(places):
    places = places.astype(f32)
    frequency = rope_base ** (-(jnp.arange(HALF, dtype=jnp.int32).astype(f32) * 2.0 / HEAD_DIM))
    angles = places[:, None] * frequency[None, :]
    cosine, sine = jnp.cos(angles), jnp.sin(angles)
    return jnp.concatenate([cosine, cosine], axis=1), jnp.concatenate([-sine, sine], axis=1)


def swap(head):
    return jnp.concatenate([head[:, HALF:], head[:, :HALF]], axis=1)


def ring_order(size):
    levels = 4 if size % 4 == 0 else size
    across = size // levels
    return [
        level * across + at
        for at in range(across)
        for level in (range(levels) if at % 2 == 0 else reversed(range(levels)))
    ]


def ring_shift(size, by):
    order = ring_order(size)
    return [(order[i], order[(i + by) % size]) for i in range(size)]


def ring_neighbour(by):
    size = lax.axis_size(F)
    order = ring_order(size)
    places = [order.index(f) for f in range(size)]
    at = jnp.array(places, jnp.int32)[lax.axis_index(F)]
    return jnp.array(order, jnp.int32)[(at + by) % size]


def ring_gather(shard, work=None):
    work = work or {}
    size = lax.axis_size(F)
    right, left = ring_shift(size, 1), ring_shift(size, -1)
    rows = shard.shape[0]
    cut = rows // 2
    whole = jnp.zeros((size * rows,) + shard.shape[1:], shard.dtype)

    def put(whole, block, by, first=0):
        return lax.dynamic_update_slice_in_dim(
            whole, block, ring_neighbour(by) * rows + first, 0
        )

    up = down = shard
    whole = put(whole, shard, 0)
    for step in range(1, size // 2):
        done = work[step](up) if step in work else None
        up, down = lax.ppermute(up, F, right), lax.ppermute(down, F, left)
        up, down = tied(up, down, done)
        whole = put(put(whole, up, -step), down, step)
    done = work[size // 2](up) if size // 2 in work else None
    up, down = lax.ppermute(up[:cut], F, right), lax.ppermute(down[cut:], F, left)
    up, down = tied(up, down, done)
    return put(put(whole, up, size // 2), down, size // 2, cut)


def ring_scatter(terms, ties=None):
    ties = ties or {}
    size = lax.axis_size(F)
    right, left = ring_shift(size, 1), ring_shift(size, -1)
    half = size // 2
    rows = terms.shape[0] // size
    cut = rows // 2

    def block(by):
        return lax.dynamic_slice_in_dim(terms, ring_neighbour(by) * rows, rows, 0)

    opposite = block(half).astype(bf16)
    up, down = opposite[:cut], opposite[cut:]
    for step in range(half - 1, 0, -1):
        up, down = lax.ppermute(up, F, right), lax.ppermute(down, F, left)
        plus, minus = block(step).astype(f32), block(-step).astype(f32)
        if step == half - 1:
            plus = jnp.concatenate([plus[:cut] + up.astype(f32), plus[cut:]])
            minus = jnp.concatenate([minus[:cut], minus[cut:] + down.astype(f32)])
        else:
            plus, minus = plus + up.astype(f32), minus + down.astype(f32)
        up, down = tied(plus.astype(bf16), minus.astype(bf16), ties.get(step))
    up, down = lax.ppermute(up, F, right), lax.ppermute(down, F, left)
    up, down = tied(up, down, ties.get(0))
    return block(0).astype(f32) + up.astype(f32) + down.astype(f32)


def tied(up, down, tie):
    if tie is None:
        return up, down
    return lax.optimization_barrier((up, down, tie))[:2]


def pick(blocks, index):
    return lax.dynamic_index_in_dim(blocks, index, 0, keepdims=False)


def swap_blocks(blocks, axis):
    return lax.all_to_all(blocks, axis, split_axis=0, concat_axis=0, tiled=True)


def sibling(value):
    return lax.ppermute(value, E, [(e, e ^ 1) for e in range(lax.axis_size(E))])


def along_y(value, by):
    size = lax.axis_size(E)
    return lax.ppermute(value, E, [(e, (e + 2 * by) % size) for e in range(size)])


def gather_e(block):
    size, at = lax.axis_size(E), lax.axis_index(E)
    levels, rows = size // 2, block.shape[0]
    whole = jnp.zeros((size * rows,) + block.shape[1:], block.dtype)
    for by in range(levels):
        came = along_y(block, by) if by else block
        source = 2 * ((at // 2 - by) % levels) + at % 2
        whole = lax.dynamic_update_slice_in_dim(whole, came, source * rows, 0)
        whole = lax.dynamic_update_slice_in_dim(whole, sibling(came), (source ^ 1) * rows, 0)
    return whole


def reduce_e(blocks):
    size, at = lax.axis_size(E), lax.axis_index(E)
    levels, core = size // 2, at % 2
    blocks = blocks.reshape((levels, 2) + blocks.shape[1:])
    mine = lax.dynamic_index_in_dim(blocks, core, 1, keepdims=False)
    theirs = lax.dynamic_index_in_dim(blocks, 1 - core, 1, keepdims=False)
    mine = mine + sibling(theirs.astype(bf16)).astype(f32)
    total = pick(mine, at // 2)
    for by in range(1, levels):
        total = total + along_y(pick(mine, (at // 2 + by) % levels).astype(bf16), by).astype(f32)
    return total


def after(value, *others):
    return lax.optimization_barrier((value,) + others)[0]


def shards(
    tokens,
    expert_ids,
    w_query,
    b_query,
    w_key,
    b_key,
    w_value,
    b_value,
    w_output,
    attn_gain,
    ffn_gain,
    w_router,
    shared_gate,
    shared_wgate,
    shared_wup,
    shared_wdown,
    expert_wgate,
    expert_wup,
    expert_wdown,
    cotangent,
):
    n_e, n_f = lax.axis_size(E), lax.axis_size(F)
    devices = n_e * n_f
    at_e, at_f = lax.axis_index(E), lax.axis_index(F)
    rows, width = tokens.shape
    seq = rows * n_f
    slab = width // n_f
    part = width // devices
    heads = HEADS // n_f
    experts, top = w_router.shape[1], expert_ids.shape[1]
    own = experts // n_e
    per_expert = expert_wgate.shape[2] // n_f
    per_shared = shared_wdown.shape[0]
    hidden_own = own * per_expert + per_shared
    score_scale = HEAD_DIM ** (-0.5)

    small = jnp.concatenate(
        [
            jnp.stack([b_query, b_key, b_value, attn_gain, ffn_gain, shared_gate]).astype(bf16),
            w_router.T.astype(bf16),
            expert_ids.T.astype(bf16).reshape(-1, part),
        ]
    )
    small_all = swap_blocks(jnp.broadcast_to(small, (devices,) + small.shape), EF)
    vectors = small_all[:, : 6 + experts].transpose(1, 0, 2).reshape(6 + experts, width)
    ids_all = small_all[:, 6 + experts :].reshape(n_e, n_f, top, rows)

    def ids_of(e):
        return pick(ids_all, e).transpose(0, 2, 1).reshape(seq, top)

    biases = lax.dynamic_slice_in_dim(vectors[:3], at_f * slab, slab, 1).astype(f32)
    gain_one = vectors[3].astype(f32)
    gain_two = vectors[4].astype(f32)
    route_rows = vectors[5:]

    w_out = lax.all_gather(w_output.astype(bf16), EF, axis=0, tiled=True)
    qkv_own = jnp.stack([w_query, w_key, w_value]).astype(bf16).reshape(3, part, n_f, slab)
    qkv_sent = qkv_own.transpose(2, 1, 0, 3).reshape(n_f, part, 3 * slab)
    qkv_own = swap_blocks(qkv_sent, F)
    w_qkv = gather_e(qkv_own.reshape(n_f * part, 3 * slab))

    def routed_blocks(expert_weight):
        routed = expert_weight.astype(bf16).transpose(0, 2, 1).reshape(own, n_f, per_expert, slab)
        return routed.transpose(1, 0, 2, 3).reshape(n_f, own * per_expert, slab)

    def shared_slabs(anchor):
        two = jnp.stack([after(shared_wgate, anchor), shared_wup]).astype(bf16)
        two = two.reshape(2, part, n_e, n_f * per_shared).transpose(2, 0, 1, 3)
        return two.reshape(n_e, 2 * part, n_f * per_shared)

    routed_down = expert_wdown.astype(bf16).reshape(own, n_f, per_expert, slab)
    routed_down = routed_down.transpose(1, 0, 2, 3).reshape(n_f, own * per_expert, slab)

    def full_width(blocks):
        return blocks.transpose(1, 0, 2).reshape(blocks.shape[1], width)

    def gate_like(mine):
        routed = full_width(mine[:, : own * per_expert])
        shared = mine[:, own * per_expert :].reshape(n_f, per_shared, n_e, part)
        shared = shared.transpose(1, 2, 0, 3).reshape(per_shared, width)
        return jnp.concatenate([routed, shared])

    def both_levels(mine):
        return lax.all_gather(mine, E, axis=0, tiled=True, axis_index_groups=along_levels)

    levels = n_e // 2
    along_levels = [[2 * level + core for level in range(levels)] for core in range(2)]
    made = {}

    def work_one(sent):
        made["shared"] = shared_slabs(sent)
        return made["shared"], qkv_sent

    def work_two(sent):
        made["gate"] = routed_blocks(after(expert_wgate, sent))
        made["up"] = routed_blocks(after(expert_wup, sent))
        return made["gate"], made["up"]

    def work_three(sent):
        two = swap_blocks(made["shared"], E).reshape(n_e, 2, part, n_f * per_shared)
        two = after(two, sent).transpose(1, 3, 0, 2)
        made["two"] = two.reshape(2, n_f, per_shared, slab)
        return made["two"], qkv_own

    def work_four(sent):
        gate, up = after((made["gate"], made["up"]), sent)
        made["both"] = jnp.concatenate([gate, made["two"][0], up, made["two"][1]], axis=1)
        return made["both"], routed_down

    x_all = ring_gather(
        tokens, {1: work_one, 2: work_two, n_f // 2 - 1: work_three, n_f // 2: work_four}
    )
    both_raw = swap_blocks(after(made["both"], x_all), F)
    g_all = lax.all_gather(after(cotangent, qkv_own), F, axis=0, tiled=True)

    blocks = own + 1
    column = jnp.arange(levels * hidden_own, dtype=jnp.int32)
    block_of = (2 * (column // hidden_own) + at_e % 2) * blocks + jnp.minimum(
        (column % hidden_own) // per_expert, own
    )
    spread = (jnp.arange(n_e * blocks, dtype=jnp.int32)[:, None] == block_of[None, :]).astype(f32)

    x_wide = x_all.astype(f32)
    x_hat = x_wide * inverse_rms(x_wide)
    normed = (x_hat * gain_one).astype(bf16)
    places = jnp.arange(seq, dtype=jnp.int32)
    cosine, sine = rope_tables(places)
    lin = product(normed, w_qkv)
    causal = places[:, None] >= places[None, :]
    saved, mixed_parts = [], []
    for h in range(heads):
        at = h * HEAD_DIM
        q_lin, k_lin, v_lin = [
            lin[:, i * slab + at : i * slab + at + HEAD_DIM] + biases[i, at : at + HEAD_DIM]
            for i in range(3)
        ]
        q = ((q_lin * cosine + swap(q_lin) * sine) * score_scale).astype(bf16)
        k = (k_lin * cosine + swap(k_lin) * sine).astype(bf16)
        v = v_lin.astype(bf16)
        scores = jnp.where(causal, product_t(q, k), -1e30)
        top_score = jnp.max(scores, axis=-1, keepdims=True)
        log_total = top_score + jnp.log(
            jnp.sum(jnp.exp(scores - top_score), axis=-1, keepdims=True)
        )
        probs = jnp.exp(scores - log_total)
        mixed_parts.append(product(probs.astype(bf16), v).astype(bf16))
        saved.append((q, k, v, probs))
    mixed = jnp.concatenate(mixed_parts, axis=1)
    mixed = after(mixed, both_raw)
    mixed_own = swap_blocks(mixed.reshape(n_f, rows, slab), F)
    down_raw = swap_blocks(after(routed_down, mixed_own), F)
    gate_mine = gate_like(both_raw[:, :hidden_own])
    mixed_own = after(mixed_own, gate_mine)
    mixed_own = mixed_own.transpose(1, 0, 2).reshape(rows, width)
    hidden = tokens.astype(f32) + product(mixed_own, w_out)

    ffn_own = (hidden * inverse_rms(hidden) * gain_two).astype(bf16)
    def work_ffn(sent):
        made["up"] = gate_like(after(both_raw, sent)[:, hidden_own:])
        return made["up"]

    w_gate = both_levels(gate_mine)
    ffn_all = ring_gather(ffn_own, {1: work_ffn, n_f // 2 - 1: lambda sent: down_raw})
    w_up = both_levels(made["up"])
    down_mine = jnp.concatenate([full_width(down_raw), shared_wdown.astype(bf16)])
    w_down = both_levels(down_mine)
    ffn_both = jnp.concatenate([ffn_all, sibling(ffn_all)])
    g_both = jnp.concatenate([g_all, sibling(g_all)])

    named = jnp.arange(experts, dtype=jnp.int32).astype(bf16)
    ids = jnp.concatenate([ids_of(at_e), ids_of(at_e ^ 1)])
    selected = jnp.sum((ids[:, :, None] == named).astype(f32), axis=1)
    logits = product_t(ffn_both, route_rows)
    logit_exp = jnp.exp(logits[:, 1:] - jnp.max(logits[:, 1:], axis=-1, keepdims=True))
    route_probs = logit_exp / jnp.sum(logit_exp, axis=-1, keepdims=True)
    shared_scale = jax.nn.sigmoid(logits[:, :1])
    gates = jnp.concatenate(
        [
            (route_probs * selected).reshape(2 * seq, n_e, own),
            jnp.broadcast_to(shared_scale[:, None, :], (2 * seq, n_e, 1)),
        ],
        axis=2,
    ).reshape(2 * seq, n_e * blocks)
    scale = dot(gates, spread, 1, 0, highest)
    pre_gate = product_t(ffn_both, w_gate)
    pre_up = product_t(ffn_both, w_up)
    sig = jax.nn.sigmoid(pre_gate)
    silu = pre_gate * sig
    slope = sig * (1.0 + pre_gate * (1.0 - sig))
    mid = (silu * pre_up).astype(bf16).astype(f32)
    mid_scaled = (mid * scale).astype(bf16)

    def over_levels(grad):
        return lax.psum_scatter(
            grad, E, scatter_dimension=0, tiled=True, axis_index_groups=along_levels
        )

    d_down_all = contract(mid_scaled, g_both).astype(bf16)
    def by_slab(grad):
        return grad.reshape(grad.shape[0], n_f, slab).transpose(1, 0, 2)

    def gate_slabs(grad):
        routed, shared = grad[: own * per_expert], grad[own * per_expert :]
        shared = shared.reshape(per_shared, n_e, n_f, part).transpose(2, 0, 1, 3)
        shared = shared.reshape(n_f, per_shared, slab)
        return jnp.concatenate([by_slab(routed), shared], axis=1)

    def return_routed(back):
        back = back.reshape(n_f, own, per_expert, slab).transpose(1, 0, 2, 3)
        return back.reshape(own, n_f * per_expert, slab)

    def return_gate(back):
        return return_routed(back[:, : own * per_expert]).transpose(0, 2, 1).astype(f32)

    mid_grad = product_t(after(g_both, d_down_all), w_down)
    sums = dot(spread, mid * mid_grad, 1, 1, highest)
    scaled = mid_grad * scale
    gate_grad = (scaled * pre_up * slope).astype(bf16)
    up_grad = (scaled * silu).astype(bf16)

    d_down = over_levels(d_down_all)
    d_gate_all = contract(gate_grad, ffn_both).astype(bf16)
    d_up_all = contract(up_grad, ffn_both).astype(bf16)
    gate_grad, up_grad = lax.optimization_barrier((gate_grad, up_grad, d_gate_all, d_up_all))[:2]

    def input_grad(first):
        rows_of = slice(first, first + seq)
        return product(gate_grad[rows_of], w_gate) + product(up_grad[rows_of], w_up)

    from_sibling = sibling(input_grad(seq).astype(bf16))
    gate_sums = sums[:, :seq] + sibling(sums[:, seq:])
    gate_sums = gate_sums.reshape(n_e * blocks, n_f, rows).transpose(1, 0, 2)
    terms = (input_grad(0) + from_sibling.astype(f32)).astype(bf16)
    gate_sums = jnp.sum(swap_blocks(gate_sums, F), axis=0)
    d_down = after(d_down, terms)
    d_down_back = swap_blocks(after(by_slab(d_down[: own * per_expert]), gate_sums), F)
    d_gate, d_up = over_levels(d_gate_all), over_levels(d_up_all)
    moe_sibling = sibling(product(after(mid_scaled, terms)[seq:], w_down).astype(bf16))
    moe = (product(mid_scaled[:seq], w_down) + moe_sibling.astype(f32)).astype(bf16)
    d_expert_down = return_routed(d_down_back).astype(f32)
    ffn_grad = ring_scatter(
        terms, {3: (gate_sums, moe_sibling), 2: moe, 1: d_expert_down}
    )
    gate_sums = gate_sums.T.reshape(rows, n_e, blocks)

    def mine(table):
        return lax.dynamic_slice_in_dim(table, at_f * rows, rows, 0)

    probs_own, shared_own, selected_own = mine(route_probs), mine(shared_scale), mine(selected)
    prob_grad = gate_sums[:, :, :own].reshape(rows, experts) * selected_own
    logit_grad = probs_own * (
        prob_grad - jnp.sum(probs_own * prob_grad, axis=-1, keepdims=True)
    )
    weight_grad = (
        jnp.sum(gate_sums[:, :, own], axis=1, keepdims=True) * shared_own * (1.0 - shared_own)
    )
    route_grad = jnp.concatenate([weight_grad, logit_grad], axis=1)
    d_route = dot(route_grad, ffn_own.astype(f32), 0, 0, highest)
    ffn_grad = ffn_grad + dot(route_grad, route_rows.astype(f32), 1, 0, highest)
    hidden_back, hidden_hat = norm_back(hidden, gain_two, ffn_grad)
    d_gain_two = jnp.sum(ffn_grad * hidden_hat, axis=0)
    hidden_grad = cotangent.astype(f32) + hidden_back

    hidden_low = hidden_grad.astype(bf16)
    mixed_grad = product_t(hidden_low, w_out).astype(bf16).reshape(rows, n_f, slab)
    mixed_grad = swap_blocks(mixed_grad.transpose(1, 0, 2), F)
    gate_back = swap_blocks(after(gate_slabs(d_gate), mixed_grad), F)
    up_back = swap_blocks(after(gate_slabs(d_up), gate_back), F)
    mixed_grad = mixed_grad.reshape(seq, slab)
    hidden_low = lax.all_gather(after(hidden_low, d_up), F, axis=0, tiled=True)
    moe = lax.psum_scatter(after(moe, hidden_low), F, scatter_dimension=0, tiled=True)
    output = (hidden + moe.astype(f32)).astype(bf16)
    d_out = contract(mixed, hidden_low)
    lin_grads = [[], [], []]
    for h in range(heads):
        q, k, v, probs = saved[h]
        out_grad = mixed_grad[:, h * HEAD_DIM : (h + 1) * HEAD_DIM]
        p_grad = product_t(out_grad, v)
        delta = jnp.sum(probs * p_grad, axis=-1, keepdims=True)
        s_grad = (probs * (p_grad - delta)).astype(bf16)
        dq = product(s_grad, k) * score_scale
        dk = contract(s_grad, q)
        lin_grads[0].append((dq * cosine - swap(dq) * sine).astype(bf16))
        lin_grads[1].append((dk * cosine - swap(dk) * sine).astype(bf16))
        lin_grads[2].append(contract(probs.astype(bf16), out_grad).astype(bf16))
    lin_grad = jnp.concatenate(lin_grads[0] + lin_grads[1] + lin_grads[2], axis=1)
    normed_part = product_t(lin_grad, w_qkv).astype(bf16)
    d_qkv = contract(normed, lin_grad)
    d_expert_gate, d_expert_up = return_gate(gate_back), return_gate(up_back)
    normed_grad = ring_scatter(normed_part, {3: d_qkv, 2: d_expert_gate, 0: up_back})
    d_bias = jnp.sum(lin_grad.astype(f32), axis=0).reshape(3, slab)
    d_gain_one = jnp.sum(d_qkv * w_qkv.astype(f32), axis=1) / gain_one
    token_back, unused = norm_back(tokens.astype(f32), gain_one, normed_grad)
    token_grad = (hidden_grad + token_back).astype(bf16)

    d_shared_down = d_down[own * per_expert :].astype(f32)
    shared_two = jnp.stack([gate_back[:, own * per_expert :], up_back[:, own * per_expert :]])
    shared_two = shared_two.reshape(2, n_f * per_shared, slab).transpose(0, 2, 1)
    shared_two = shared_two.reshape(2, n_e, part, n_f * per_shared).transpose(1, 0, 2, 3)
    shared_two = swap_blocks(shared_two.reshape(n_e, 2 * part, n_f * per_shared), E)
    shared_two = shared_two.reshape(n_e, 2, part, n_f * per_shared).transpose(1, 2, 0, 3)
    shared_two = shared_two.reshape(2, part, devices * per_shared).astype(f32)

    from_heads = [(e * n_f + f, n_e * f + e) for e in range(n_e) for f in range(n_f)]
    d_out = reduce_e(d_out.reshape(n_e, part, width)).astype(bf16)
    d_wout = lax.ppermute(d_out, EF, from_heads).astype(f32)
    d_qkv = reduce_e(d_qkv.reshape(n_e, n_f * part, 3 * slab)).astype(bf16)
    d_qkv = swap_blocks(d_qkv.reshape(n_f, part, 3 * slab), F)
    d_qkv = d_qkv.reshape(n_f, part, 3, slab).transpose(2, 1, 0, 3).reshape(3, part, width)
    d_qkv = d_qkv.astype(f32)

    bias_rows = lax.dynamic_update_slice_in_dim(
        jnp.zeros((3, width), f32), d_bias, at_f * slab, 1
    )
    d_small = jnp.concatenate([bias_rows, d_gain_one[None], d_gain_two[None], d_route])
    d_small = d_small.reshape(6 + experts, devices, part).transpose(1, 0, 2)
    d_small = jnp.sum(swap_blocks(d_small, EF), axis=0)

    return (
        output,
        token_grad,
        d_qkv[0],
        d_small[0],
        d_qkv[1],
        d_small[1],
        d_qkv[2],
        d_small[2],
        d_wout,
        d_small[3],
        d_small[4],
        d_small[6:].T,
        d_small[5],
        shared_two[0],
        shared_two[1],
        d_shared_down,
        d_expert_gate,
        d_expert_up,
        d_expert_down,
    )


def solution(mesh):
    matrix, vector = P(EF, None), P(EF)
    wide, tall = P(E, F, None), P(E, None, F)
    in_specs = (matrix, matrix) + (matrix, vector) * 3 + (matrix, vector, vector, matrix, vector)
    in_specs = in_specs + (matrix,) * 3 + (wide, wide, tall, matrix)
    out_specs = (matrix, matrix) + (matrix, vector) * 3 + (matrix, vector, vector, matrix, vector)
    out_specs = out_specs + (matrix,) * 3 + (wide, wide, tall)
    return jax.shard_map(shards, mesh=mesh, in_specs=in_specs, out_specs=out_specs, check_vma=False)
```

```python
import jax
import jax.numpy as jnp
from jax import lax
from jax.sharding import PartitionSpec as P

HEADS = 16
HEAD_DIM = 128
HALF = HEAD_DIM // 2

E = "expert"
F = "fsdp"
EF = (E, F)

norm_eps = 1e-06
rope_base = 1000000.0
highest = lax.Precision.HIGHEST
bf16 = jnp.bfloat16
f32 = jnp.float32


def dot(left, right, left_dim, right_dim, precision=None):
    return lax.dot_general(
        left,
        right,
        (((left_dim,), (right_dim,)), ((), ())),
        precision=precision,
        preferred_element_type=f32,
    )


def product(left, right):
    return dot(left, right, 1, 0)


def product_t(left, right):
    return dot(left, right, 1, 1)


def contract(left, right):
    return dot(left, right, 0, 0)


def inverse_rms(rows):
    return lax.rsqrt(jnp.mean(rows * rows, axis=-1, keepdims=True) + norm_eps)


def norm_back(rows, gain, grad):
    factor = inverse_rms(rows)
    scaled = grad * gain
    along = jnp.mean(rows * scaled, axis=-1, keepdims=True)
    return factor * scaled - rows * (factor * factor * factor * along), rows * factor


def rope_tables(places):
    places = places.astype(f32)
    frequency = rope_base ** (-(jnp.arange(HALF, dtype=jnp.int32).astype(f32) * 2.0 / HEAD_DIM))
    angles = places[:, None] * frequency[None, :]
    cosine, sine = jnp.cos(angles), jnp.sin(angles)
    return jnp.concatenate([cosine, cosine], axis=1), jnp.concatenate([-sine, sine], axis=1)


def swap(head):
    return jnp.concatenate([head[:, HALF:], head[:, :HALF]], axis=1)


def ring_order(size):
    levels = 4 if size % 4 == 0 else size
    across = size // levels
    return [
        level * across + at
        for at in range(across)
        for level in (range(levels) if at % 2 == 0 else reversed(range(levels)))
    ]


def ring_shift(size, by):
    order = ring_order(size)
    return [(order[i], order[(i + by) % size]) for i in range(size)]


def ring_neighbour(by):
    size = lax.axis_size(F)
    order = ring_order(size)
    places = [order.index(f) for f in range(size)]
    at = jnp.array(places, jnp.int32)[lax.axis_index(F)]
    return jnp.array(order, jnp.int32)[(at + by) % size]


def ring_gather(shard, work=None):
    work = work or {}
    size = lax.axis_size(F)
    right, left = ring_shift(size, 1), ring_shift(size, -1)
    rows = shard.shape[0]
    cut = rows // 2
    whole = jnp.zeros((size * rows,) + shard.shape[1:], shard.dtype)

    def put(whole, block, by, first=0):
        return lax.dynamic_update_slice_in_dim(
            whole, block, ring_neighbour(by) * rows + first, 0
        )

    up = down = shard
    whole = put(whole, shard, 0)
    for step in range(1, size // 2):
        done = work[step](up) if step in work else None
        up, down = lax.ppermute(up, F, right), lax.ppermute(down, F, left)
        up, down = tied(up, down, done)
        whole = put(put(whole, up, -step), down, step)
    done = work[size // 2](up) if size // 2 in work else None
    up, down = lax.ppermute(up[:cut], F, right), lax.ppermute(down[cut:], F, left)
    up, down = tied(up, down, done)
    return put(put(whole, up, size // 2), down, size // 2, cut)


def ring_scatter(terms, ties=None):
    ties = ties or {}
    size = lax.axis_size(F)
    right, left = ring_shift(size, 1), ring_shift(size, -1)
    half = size // 2
    rows = terms.shape[0] // size
    cut = rows // 2

    def block(by):
        return lax.dynamic_slice_in_dim(terms, ring_neighbour(by) * rows, rows, 0)

    opposite = block(half).astype(bf16)
    up, down = opposite[:cut], opposite[cut:]
    for step in range(half - 1, 0, -1):
        up, down = lax.ppermute(up, F, right), lax.ppermute(down, F, left)
        plus, minus = block(step).astype(f32), block(-step).astype(f32)
        if step == half - 1:
            plus = jnp.concatenate([plus[:cut] + up.astype(f32), plus[cut:]])
            minus = jnp.concatenate([minus[:cut], minus[cut:] + down.astype(f32)])
        else:
            plus, minus = plus + up.astype(f32), minus + down.astype(f32)
        up, down = tied(plus.astype(bf16), minus.astype(bf16), ties.get(step))
    up, down = lax.ppermute(up, F, right), lax.ppermute(down, F, left)
    up, down = tied(up, down, ties.get(0))
    return block(0).astype(f32) + up.astype(f32) + down.astype(f32)


def tied(up, down, tie):
    if tie is None:
        return up, down
    return lax.optimization_barrier((up, down, tie))[:2]


def pick(blocks, index):
    return lax.dynamic_index_in_dim(blocks, index, 0, keepdims=False)


def swap_blocks(blocks, axis):
    return lax.all_to_all(blocks, axis, split_axis=0, concat_axis=0, tiled=True)


def sibling(value):
    return lax.ppermute(value, E, [(e, e ^ 1) for e in range(lax.axis_size(E))])


def along_y(value, by):
    size = lax.axis_size(E)
    return lax.ppermute(value, E, [(e, (e + 2 * by) % size) for e in range(size)])


def gather_e(block):
    size, at = lax.axis_size(E), lax.axis_index(E)
    levels, rows = size // 2, block.shape[0]
    whole = jnp.zeros((size * rows,) + block.shape[1:], block.dtype)
    for by in range(levels):
        came = along_y(block, by) if by else block
        source = 2 * ((at // 2 - by) % levels) + at % 2
        whole = lax.dynamic_update_slice_in_dim(whole, came, source * rows, 0)
        whole = lax.dynamic_update_slice_in_dim(whole, sibling(came), (source ^ 1) * rows, 0)
    return whole


def after(value, *others):
    return lax.optimization_barrier((value,) + others)[0]


def shards(
    tokens,
    expert_ids,
    w_query,
    b_query,
    w_key,
    b_key,
    w_value,
    b_value,
    w_output,
    attn_gain,
    ffn_gain,
    w_router,
    shared_gate,
    shared_wgate,
    shared_wup,
    shared_wdown,
    expert_wgate,
    expert_wup,
    expert_wdown,
    cotangent,
):
    n_e, n_f = lax.axis_size(E), lax.axis_size(F)
    devices = n_e * n_f
    at_e, at_f = lax.axis_index(E), lax.axis_index(F)
    rows, width = tokens.shape
    seq = rows * n_f
    slab = width // n_f
    part = width // devices
    heads = HEADS // n_f
    experts, top = w_router.shape[1], expert_ids.shape[1]
    own = experts // n_e
    per_expert = expert_wgate.shape[2] // n_f
    per_shared = shared_wdown.shape[0]
    hidden_own = own * per_expert + per_shared
    score_scale = HEAD_DIM ** (-0.5)

    small = jnp.concatenate(
        [
            jnp.stack([b_query, b_key, b_value, attn_gain, ffn_gain, shared_gate]).astype(bf16),
            w_router.T.astype(bf16),
            expert_ids.T.astype(bf16).reshape(-1, part),
        ]
    )
    small_all = swap_blocks(jnp.broadcast_to(small, (devices,) + small.shape), EF)
    vectors = small_all[:, : 6 + experts].transpose(1, 0, 2).reshape(6 + experts, width)
    ids_all = small_all[:, 6 + experts :].reshape(n_e, n_f, top, rows)

    def ids_of(e):
        return pick(ids_all, e).transpose(0, 2, 1).reshape(seq, top)

    biases = lax.dynamic_slice_in_dim(vectors[:3], at_f * slab, slab, 1).astype(f32)
    gain_one = vectors[3].astype(f32)
    gain_two = vectors[4].astype(f32)
    route_rows = vectors[5:]

    w_out = lax.all_gather(w_output.astype(bf16), EF, axis=0, tiled=True)
    qkv_sent = jnp.concatenate(
        [
            jnp.concatenate([w[:, f * slab : (f + 1) * slab] for w in (w_query, w_key, w_value)], 1)
            for f in range(n_f)
        ]
    ).astype(bf16)
    qkv_sent = qkv_sent.reshape(n_f, part, 3 * slab)
    qkv_own = swap_blocks(qkv_sent, F)
    w_qkv = gather_e(qkv_own.reshape(n_f * part, 3 * slab))

    def routed_blocks(expert_weight):
        routed = expert_weight.astype(bf16).transpose(0, 2, 1).reshape(own, n_f, per_expert, slab)
        return routed.transpose(1, 0, 2, 3).reshape(n_f, own * per_expert, slab)

    def shared_slabs(anchor):
        columns = n_f * per_shared
        gate = after(shared_wgate, anchor)
        two = jnp.concatenate(
            [w[:, e * columns : (e + 1) * columns] for e in range(n_e) for w in (gate, shared_wup)]
        )
        return two.astype(bf16).reshape(n_e, 2 * part, columns)

    routed_down = expert_wdown.astype(bf16).reshape(own, n_f, per_expert, slab)
    routed_down = routed_down.transpose(1, 0, 2, 3).reshape(n_f, own * per_expert, slab)

    def full_width(blocks):
        return blocks.transpose(1, 0, 2).reshape(blocks.shape[1], width)

    def gate_like(mine):
        routed = full_width(mine[:, : own * per_expert])
        shared = mine[:, own * per_expert :].reshape(n_f, per_shared, n_e, part)
        shared = shared.transpose(1, 2, 0, 3).reshape(per_shared, width)
        return jnp.concatenate([routed, shared])

    def both_levels(mine):
        return lax.all_gather(mine, E, axis=0, tiled=True, axis_index_groups=along_levels)

    levels = n_e // 2
    along_levels = [[2 * level + core for level in range(levels)] for core in range(2)]
    made = {}

    def work_one(sent):
        made["shared"] = shared_slabs(sent)
        return made["shared"], qkv_sent

    def work_two(sent):
        made["gate"] = routed_blocks(after(expert_wgate, sent))
        made["up"] = routed_blocks(after(expert_wup, sent))
        return made["gate"], made["up"]

    def work_three(sent):
        two = swap_blocks(made["shared"], E).reshape(n_e, 2, part, n_f * per_shared)
        two = after(two, sent).transpose(1, 3, 0, 2)
        made["two"] = two.reshape(2, n_f, per_shared, slab)
        return made["two"], qkv_own

    def work_four(sent):
        gate, up = after((made["gate"], made["up"]), sent)
        made["both"] = jnp.concatenate([gate, made["two"][0], up, made["two"][1]], axis=1)
        return made["both"], routed_down

    x_all = ring_gather(
        tokens, {1: work_one, 2: work_two, n_f // 2 - 1: work_three, n_f // 2: work_four}
    )
    both_raw = swap_blocks(after(made["both"], x_all), F)
    g_all = lax.all_gather(after(cotangent, qkv_own), F, axis=0, tiled=True)

    blocks = own + 1
    column = jnp.arange(levels * hidden_own, dtype=jnp.int32)
    block_of = (2 * (column // hidden_own) + at_e % 2) * blocks + jnp.minimum(
        (column % hidden_own) // per_expert, own
    )
    spread = (jnp.arange(n_e * blocks, dtype=jnp.int32)[:, None] == block_of[None, :]).astype(f32)

    x_wide = x_all.astype(f32)
    x_hat = x_wide * inverse_rms(x_wide)
    normed = (x_hat * gain_one).astype(bf16)
    places = jnp.arange(seq, dtype=jnp.int32)
    cosine, sine = rope_tables(places)
    lin = product(normed, w_qkv)
    causal = places[:, None] >= places[None, :]
    saved, mixed_parts = [], []
    for h in range(heads):
        at = h * HEAD_DIM
        q_lin, k_lin, v_lin = [
            lin[:, i * slab + at : i * slab + at + HEAD_DIM] + biases[i, at : at + HEAD_DIM]
            for i in range(3)
        ]
        q = ((q_lin * cosine + swap(q_lin) * sine) * score_scale).astype(bf16)
        k = (k_lin * cosine + swap(k_lin) * sine).astype(bf16)
        v = v_lin.astype(bf16)
        scores = jnp.where(causal, product_t(q, k), -1e30)
        top_score = jnp.max(scores, axis=-1, keepdims=True)
        log_total = top_score + jnp.log(
            jnp.sum(jnp.exp(scores - top_score), axis=-1, keepdims=True)
        )
        probs = jnp.exp(scores - log_total)
        mixed_parts.append(product(probs.astype(bf16), v).astype(bf16))
        saved.append((q, k, v, probs))
    mixed = jnp.concatenate(mixed_parts, axis=1)
    mixed = after(mixed, both_raw)
    mixed_own = swap_blocks(mixed.reshape(n_f, rows, slab), F)
    down_raw = swap_blocks(after(routed_down, mixed_own), F)
    gate_mine = gate_like(both_raw[:, :hidden_own])
    mixed_own = after(mixed_own, gate_mine)
    mixed_own = mixed_own.transpose(1, 0, 2).reshape(rows, width)
    hidden = tokens.astype(f32) + product(mixed_own, w_out)

    ffn_own = (hidden * inverse_rms(hidden) * gain_two).astype(bf16)
    def work_ffn(sent):
        made["up"] = gate_like(after(both_raw, sent)[:, hidden_own:])
        return made["up"]

    w_gate = both_levels(gate_mine)
    ffn_all = ring_gather(ffn_own, {1: work_ffn, n_f // 2 - 1: lambda sent: down_raw})
    w_up = both_levels(made["up"])
    down_mine = jnp.concatenate([full_width(down_raw), shared_wdown.astype(bf16)])
    w_down = both_levels(down_mine)
    ffn_both = jnp.concatenate([ffn_all, sibling(ffn_all)])
    g_both = jnp.concatenate([g_all, sibling(g_all)])

    named = jnp.arange(experts, dtype=jnp.int32).astype(bf16)
    ids = jnp.concatenate([ids_of(at_e), ids_of(at_e ^ 1)])
    selected = jnp.sum((ids[:, :, None] == named).astype(f32), axis=1)
    logits = product_t(ffn_both, route_rows)
    logit_exp = jnp.exp(logits[:, 1:] - jnp.max(logits[:, 1:], axis=-1, keepdims=True))
    route_probs = logit_exp / jnp.sum(logit_exp, axis=-1, keepdims=True)
    shared_scale = jax.nn.sigmoid(logits[:, :1])
    gates = jnp.concatenate(
        [
            (route_probs * selected).reshape(2 * seq, n_e, own),
            jnp.broadcast_to(shared_scale[:, None, :], (2 * seq, n_e, 1)),
        ],
        axis=2,
    ).reshape(2 * seq, n_e * blocks)
    scale = dot(gates, spread, 1, 0, highest)
    pre_gate = product_t(ffn_both, w_gate)
    pre_up = product_t(ffn_both, w_up)
    sig = jax.nn.sigmoid(pre_gate)
    silu = pre_gate * sig
    slope = sig * (1.0 + pre_gate * (1.0 - sig))
    mid = (silu * pre_up).astype(bf16).astype(f32)
    mid_scaled = (mid * scale).astype(bf16)

    def over_levels(grad):
        return lax.psum_scatter(
            grad, E, scatter_dimension=0, tiled=True, axis_index_groups=along_levels
        )

    d_down_all = contract(mid_scaled, g_both).astype(bf16)
    def by_slab(grad):
        return grad.reshape(grad.shape[0], n_f, slab).transpose(1, 0, 2)

    def gate_slabs(grad):
        routed, shared = grad[: own * per_expert], grad[own * per_expert :]
        shared = shared.reshape(per_shared, n_e, n_f, part).transpose(2, 0, 1, 3)
        shared = shared.reshape(n_f, per_shared, slab)
        return jnp.concatenate([by_slab(routed), shared], axis=1)

    def return_routed(back):
        back = back.reshape(n_f, own, per_expert, slab).transpose(1, 0, 2, 3)
        return back.reshape(own, n_f * per_expert, slab)

    def return_gate(back):
        return return_routed(back[:, : own * per_expert]).transpose(0, 2, 1).astype(f32)

    mid_grad = product_t(after(g_both, d_down_all), w_down)
    sums = dot(spread, mid * mid_grad, 1, 1, highest)
    scaled = mid_grad * scale
    gate_grad = (scaled * pre_up * slope).astype(bf16)
    up_grad = (scaled * silu).astype(bf16)

    d_down = over_levels(d_down_all)
    d_gate_all = contract(gate_grad, ffn_both).astype(bf16)
    d_up_all = contract(up_grad, ffn_both).astype(bf16)
    gate_grad, up_grad = lax.optimization_barrier((gate_grad, up_grad, d_gate_all, d_up_all))[:2]

    def input_grad(first):
        rows_of = slice(first, first + seq)
        return product(gate_grad[rows_of], w_gate) + product(up_grad[rows_of], w_up)

    from_sibling = sibling(input_grad(seq).astype(bf16))
    gate_sums = sums[:, :seq] + sibling(sums[:, seq:])
    gate_sums = gate_sums.reshape(n_e * blocks, n_f, rows).transpose(1, 0, 2)
    terms = (input_grad(0) + from_sibling.astype(f32)).astype(bf16)
    gate_sums = jnp.sum(swap_blocks(gate_sums, F), axis=0)
    d_down = after(d_down, terms)
    d_down_back = swap_blocks(after(by_slab(d_down[: own * per_expert]), gate_sums), F)
    d_gate, d_up = over_levels(d_gate_all), over_levels(d_up_all)
    moe_sibling = sibling(product(after(mid_scaled, terms)[seq:], w_down).astype(bf16))
    moe = (product(mid_scaled[:seq], w_down) + moe_sibling.astype(f32)).astype(bf16)
    d_expert_down = return_routed(d_down_back).astype(f32)
    ffn_grad = ring_scatter(
        terms, {3: (gate_sums, moe_sibling), 2: moe, 1: d_expert_down}
    )
    gate_sums = gate_sums.T.reshape(rows, n_e, blocks)

    def mine(table):
        return lax.dynamic_slice_in_dim(table, at_f * rows, rows, 0)

    probs_own, shared_own, selected_own = mine(route_probs), mine(shared_scale), mine(selected)
    prob_grad = gate_sums[:, :, :own].reshape(rows, experts) * selected_own
    logit_grad = probs_own * (
        prob_grad - jnp.sum(probs_own * prob_grad, axis=-1, keepdims=True)
    )
    weight_grad = (
        jnp.sum(gate_sums[:, :, own], axis=1, keepdims=True) * shared_own * (1.0 - shared_own)
    )
    route_grad = jnp.concatenate([weight_grad, logit_grad], axis=1)
    d_route = dot(route_grad, ffn_own.astype(f32), 0, 0, highest)
    ffn_grad = ffn_grad + dot(route_grad, route_rows.astype(f32), 1, 0, highest)
    hidden_back, hidden_hat = norm_back(hidden, gain_two, ffn_grad)
    d_gain_two = jnp.sum(ffn_grad * hidden_hat, axis=0)
    hidden_grad = cotangent.astype(f32) + hidden_back

    hidden_low = hidden_grad.astype(bf16)
    mixed_grad = product_t(hidden_low, w_out).astype(bf16).reshape(rows, n_f, slab)
    mixed_grad = swap_blocks(mixed_grad.transpose(1, 0, 2), F)
    gate_back = swap_blocks(after(gate_slabs(d_gate), mixed_grad), F)
    up_back = swap_blocks(after(gate_slabs(d_up), gate_back), F)
    mixed_grad = mixed_grad.reshape(seq, slab)
    moe = lax.psum_scatter(after(moe, d_up, ffn_grad), F, scatter_dimension=0, tiled=True)
    output = (hidden + moe.astype(f32)).astype(bf16)
    lin_grads = [[], [], []]
    for h in range(heads):
        q, k, v, probs = saved[h]
        out_grad = mixed_grad[:, h * HEAD_DIM : (h + 1) * HEAD_DIM]
        p_grad = product_t(out_grad, v)
        delta = jnp.sum(probs * p_grad, axis=-1, keepdims=True)
        s_grad = (probs * (p_grad - delta)).astype(bf16)
        dq = product(s_grad, k) * score_scale
        dk = contract(s_grad, q)
        lin_grads[0].append((dq * cosine - swap(dq) * sine).astype(bf16))
        lin_grads[1].append((dk * cosine - swap(dk) * sine).astype(bf16))
        lin_grads[2].append(contract(probs.astype(bf16), out_grad).astype(bf16))
    lin_grad = jnp.concatenate(lin_grads[0] + lin_grads[1] + lin_grads[2], axis=1)
    normed_part = product_t(lin_grad, w_qkv).astype(bf16)
    d_qkv = contract(normed, lin_grad)
    d_expert_gate, d_expert_up = return_gate(gate_back), return_gate(up_back)
    normed_grad = ring_scatter(normed_part, {3: d_qkv, 1: gate_back})
    hidden_low = lax.all_gather(after(hidden_low, moe, normed_part), F, axis=0, tiled=True)
    d_out = contract(mixed, hidden_low)
    d_bias = jnp.sum(lin_grad.astype(f32), axis=0).reshape(3, slab)
    d_gain_one = jnp.sum(d_qkv * w_qkv.astype(f32), axis=1) / gain_one
    token_back, unused = norm_back(tokens.astype(f32), gain_one, normed_grad)
    token_grad = (hidden_grad + token_back).astype(bf16)

    d_shared_down = d_down[own * per_expert :].astype(f32)
    shared_two = jnp.stack([gate_back[:, own * per_expert :], up_back[:, own * per_expert :]])
    shared_two = shared_two.reshape(2, n_f * per_shared, slab).transpose(0, 2, 1)
    shared_two = shared_two.reshape(2, n_e, part, n_f * per_shared).transpose(1, 0, 2, 3)
    shared_two = swap_blocks(shared_two.reshape(n_e, 2 * part, n_f * per_shared), E)
    shared_two = shared_two.reshape(n_e, 2, part, n_f * per_shared).transpose(1, 2, 0, 3)
    shared_two = shared_two.reshape(2, part, devices * per_shared).astype(f32)

    from_heads = [(e * n_f + f, n_e * f + e) for e in range(n_e) for f in range(n_f)]
    d_out = lax.psum_scatter(d_out.astype(bf16), E, scatter_dimension=0, tiled=True)
    d_wout = lax.ppermute(d_out, EF, from_heads).astype(f32)
    d_qkv = lax.psum_scatter(d_qkv.astype(bf16), E, scatter_dimension=0, tiled=True)
    d_qkv = swap_blocks(d_qkv.reshape(n_f, part, 3 * slab), F)
    d_qkv = d_qkv.reshape(n_f, part, 3, slab).transpose(2, 1, 0, 3).reshape(3, part, width)
    d_qkv = d_qkv.astype(f32)

    bias_rows = lax.dynamic_update_slice_in_dim(
        jnp.zeros((3, width), f32), d_bias, at_f * slab, 1
    )
    d_small = jnp.concatenate([bias_rows, d_gain_one[None], d_gain_two[None], d_route])
    d_small = d_small.reshape(6 + experts, devices, part).transpose(1, 0, 2)
    d_small = jnp.sum(swap_blocks(d_small, EF), axis=0)

    return (
        output,
        token_grad,
        d_qkv[0],
        d_small[0],
        d_qkv[1],
        d_small[1],
        d_qkv[2],
        d_small[2],
        d_wout,
        d_small[3],
        d_small[4],
        d_small[6:].T,
        d_small[5],
        shared_two[0],
        shared_two[1],
        d_shared_down,
        d_expert_gate,
        d_expert_up,
        d_expert_down,
    )


def solution(mesh):
    matrix, vector = P(EF, None), P(EF)
    wide, tall = P(E, F, None), P(E, None, F)
    in_specs = (matrix, matrix) + (matrix, vector) * 3 + (matrix, vector, vector, matrix, vector)
    in_specs = in_specs + (matrix,) * 3 + (wide, wide, tall, matrix)
    out_specs = (matrix, matrix) + (matrix, vector) * 3 + (matrix, vector, vector, matrix, vector)
    out_specs = out_specs + (matrix,) * 3 + (wide, wide, tall)
    return jax.shard_map(shards, mesh=mesh, in_specs=in_specs, out_specs=out_specs, check_vma=False)
```

```python
import jax
import jax.numpy as jnp
from jax import lax
from jax.sharding import PartitionSpec as P

HEADS = 16
HEAD_DIM = 128
HALF = HEAD_DIM // 2

E = "expert"
F = "fsdp"
EF = (E, F)

norm_eps = 1e-06
rope_base = 1000000.0
highest = lax.Precision.HIGHEST
bf16 = jnp.bfloat16
f32 = jnp.float32


def dot(left, right, left_dim, right_dim, precision=None):
    return lax.dot_general(
        left,
        right,
        (((left_dim,), (right_dim,)), ((), ())),
        precision=precision,
        preferred_element_type=f32,
    )


def product(left, right):
    return dot(left, right, 1, 0)


def product_t(left, right):
    return dot(left, right, 1, 1)


def contract(left, right):
    return dot(left, right, 0, 0)


def inverse_rms(rows):
    return lax.rsqrt(jnp.mean(rows * rows, axis=-1, keepdims=True) + norm_eps)


def norm_back(rows, gain, grad):
    factor = inverse_rms(rows)
    scaled = grad * gain
    along = jnp.mean(rows * scaled, axis=-1, keepdims=True)
    return factor * scaled - rows * (factor * factor * factor * along), rows * factor


def rope_tables(places):
    places = places.astype(f32)
    frequency = rope_base ** (-(jnp.arange(HALF, dtype=jnp.int32).astype(f32) * 2.0 / HEAD_DIM))
    angles = places[:, None] * frequency[None, :]
    cosine, sine = jnp.cos(angles), jnp.sin(angles)
    return jnp.concatenate([cosine, cosine], axis=1), jnp.concatenate([-sine, sine], axis=1)


def swap(head):
    return jnp.concatenate([head[:, HALF:], head[:, :HALF]], axis=1)


def ring_order(size):
    levels = 4 if size % 4 == 0 else size
    across = size // levels
    return [
        level * across + at
        for at in range(across)
        for level in (range(levels) if at % 2 == 0 else reversed(range(levels)))
    ]


def ring_shift(size, by):
    order = ring_order(size)
    return [(order[i], order[(i + by) % size]) for i in range(size)]


def ring_neighbour(by):
    size = lax.axis_size(F)
    order = ring_order(size)
    places = [order.index(f) for f in range(size)]
    at = jnp.array(places, jnp.int32)[lax.axis_index(F)]
    return jnp.array(order, jnp.int32)[(at + by) % size]


def ring_gather(shard, work=None):
    work = work or {}
    size = lax.axis_size(F)
    right, left = ring_shift(size, 1), ring_shift(size, -1)
    rows = shard.shape[0]
    cut = rows // 2
    whole = jnp.zeros((size * rows,) + shard.shape[1:], shard.dtype)

    def put(whole, block, by, first=0):
        return lax.dynamic_update_slice_in_dim(
            whole, block, ring_neighbour(by) * rows + first, 0
        )

    up = down = shard
    whole = put(whole, shard, 0)
    for step in range(1, size // 2):
        done = work[step](up) if step in work else None
        up, down = lax.ppermute(up, F, right), lax.ppermute(down, F, left)
        up, down = tied(up, down, done)
        whole = put(put(whole, up, -step), down, step)
    done = work[size // 2](up) if size // 2 in work else None
    up, down = lax.ppermute(up[:cut], F, right), lax.ppermute(down[cut:], F, left)
    up, down = tied(up, down, done)
    return put(put(whole, up, size // 2), down, size // 2, cut)


def ring_scatter(terms, ties=None):
    ties = ties or {}
    size = lax.axis_size(F)
    right, left = ring_shift(size, 1), ring_shift(size, -1)
    half = size // 2
    rows = terms.shape[0] // size
    cut = rows // 2

    def block(by):
        return lax.dynamic_slice_in_dim(terms, ring_neighbour(by) * rows, rows, 0)

    opposite = block(half).astype(bf16)
    up, down = opposite[:cut], opposite[cut:]
    for step in range(half - 1, 0, -1):
        up, down = lax.ppermute(up, F, right), lax.ppermute(down, F, left)
        plus, minus = block(step).astype(f32), block(-step).astype(f32)
        if step == half - 1:
            plus = jnp.concatenate([plus[:cut] + up.astype(f32), plus[cut:]])
            minus = jnp.concatenate([minus[:cut], minus[cut:] + down.astype(f32)])
        else:
            plus, minus = plus + up.astype(f32), minus + down.astype(f32)
        up, down = tied(plus.astype(bf16), minus.astype(bf16), ties.get(step))
    up, down = lax.ppermute(up, F, right), lax.ppermute(down, F, left)
    up, down = tied(up, down, ties.get(0))
    return block(0).astype(f32) + up.astype(f32) + down.astype(f32)


def tied(up, down, tie):
    if tie is None:
        return up, down
    return lax.optimization_barrier((up, down, tie))[:2]


def pick(blocks, index):
    return lax.dynamic_index_in_dim(blocks, index, 0, keepdims=False)


def swap_blocks(blocks, axis):
    return lax.all_to_all(blocks, axis, split_axis=0, concat_axis=0, tiled=True)


def sibling(value):
    return lax.ppermute(value, E, [(e, e ^ 1) for e in range(lax.axis_size(E))])


def along_y(value, by):
    size = lax.axis_size(E)
    return lax.ppermute(value, E, [(e, (e + 2 * by) % size) for e in range(size)])


def gather_e(block):
    size, at = lax.axis_size(E), lax.axis_index(E)
    levels, rows = size // 2, block.shape[0]
    whole = jnp.zeros((size * rows,) + block.shape[1:], block.dtype)
    for by in range(levels):
        came = along_y(block, by) if by else block
        source = 2 * ((at // 2 - by) % levels) + at % 2
        whole = lax.dynamic_update_slice_in_dim(whole, came, source * rows, 0)
        whole = lax.dynamic_update_slice_in_dim(whole, sibling(came), (source ^ 1) * rows, 0)
    return whole


def after(value, *others):
    return lax.optimization_barrier((value,) + others)[0]


def shards(
    tokens,
    expert_ids,
    w_query,
    b_query,
    w_key,
    b_key,
    w_value,
    b_value,
    w_output,
    attn_gain,
    ffn_gain,
    w_router,
    shared_gate,
    shared_wgate,
    shared_wup,
    shared_wdown,
    expert_wgate,
    expert_wup,
    expert_wdown,
    cotangent,
):
    n_e, n_f = lax.axis_size(E), lax.axis_size(F)
    devices = n_e * n_f
    at_e, at_f = lax.axis_index(E), lax.axis_index(F)
    rows, width = tokens.shape
    seq = rows * n_f
    slab = width // n_f
    part = width // devices
    heads = HEADS // n_f
    experts, top = w_router.shape[1], expert_ids.shape[1]
    own = experts // n_e
    per_expert = expert_wgate.shape[2] // n_f
    per_shared = shared_wdown.shape[0]
    hidden_own = own * per_expert + per_shared
    score_scale = HEAD_DIM ** (-0.5)

    small = jnp.concatenate(
        [
            jnp.stack([b_query, b_key, b_value, attn_gain, ffn_gain, shared_gate]).astype(bf16),
            w_router.T.astype(bf16),
            expert_ids.T.astype(bf16).reshape(-1, part),
        ]
    )
    small_all = swap_blocks(jnp.broadcast_to(small, (devices,) + small.shape), EF)
    vectors = small_all[:, : 6 + experts].transpose(1, 0, 2).reshape(6 + experts, width)
    ids_all = small_all[:, 6 + experts :].reshape(n_e, n_f, top, rows)

    def ids_of(e):
        return pick(ids_all, e).transpose(0, 2, 1).reshape(seq, top)

    biases = lax.dynamic_slice_in_dim(vectors[:3], at_f * slab, slab, 1).astype(f32)
    gain_one = vectors[3].astype(f32)
    gain_two = vectors[4].astype(f32)
    route_rows = vectors[5:]

    w_out = lax.all_gather(w_output.astype(bf16), EF, axis=0, tiled=True)
    qkv_sent = jnp.concatenate(
        [
            jnp.concatenate([w[:, f * slab : (f + 1) * slab] for w in (w_query, w_key, w_value)], 1)
            for f in range(n_f)
        ]
    ).astype(bf16)
    qkv_sent = qkv_sent.reshape(n_f, part, 3 * slab)
    qkv_own = swap_blocks(qkv_sent, F)
    w_qkv = gather_e(qkv_own.reshape(n_f * part, 3 * slab))

    def routed_blocks(expert_weight):
        routed = expert_weight.astype(bf16).transpose(0, 2, 1).reshape(own, n_f, per_expert, slab)
        return routed.transpose(1, 0, 2, 3).reshape(n_f, own * per_expert, slab)

    def shared_slabs(anchor):
        columns = n_f * per_shared
        gate = after(shared_wgate, anchor)
        two = jnp.concatenate(
            [w[:, e * columns : (e + 1) * columns] for e in range(n_e) for w in (gate, shared_wup)]
        )
        return two.astype(bf16).reshape(n_e, 2 * part, columns)

    routed_down = expert_wdown.astype(bf16).reshape(own, n_f, per_expert, slab)
    routed_down = routed_down.transpose(1, 0, 2, 3).reshape(n_f, own * per_expert, slab)

    def full_width(blocks):
        return blocks.transpose(1, 0, 2).reshape(blocks.shape[1], width)

    def gate_like(mine):
        routed = full_width(mine[:, : own * per_expert])
        shared = mine[:, own * per_expert :].reshape(n_f, per_shared, n_e, part)
        shared = shared.transpose(1, 2, 0, 3).reshape(per_shared, width)
        return jnp.concatenate([routed, shared])

    def both_levels(mine):
        return lax.all_gather(mine, E, axis=0, tiled=True, axis_index_groups=along_levels)

    levels = n_e // 2
    along_levels = [[2 * level + core for level in range(levels)] for core in range(2)]
    made = {}

    def work_one(sent):
        made["shared"] = shared_slabs(sent)
        return made["shared"], qkv_sent

    def work_two(sent):
        made["gate"] = routed_blocks(after(expert_wgate, sent))
        made["up"] = routed_blocks(after(expert_wup, sent))
        return made["gate"], made["up"]

    def work_three(sent):
        two = swap_blocks(made["shared"], E).reshape(n_e, 2, part, n_f * per_shared)
        two = after(two, sent).transpose(1, 3, 0, 2)
        made["two"] = two.reshape(2, n_f, per_shared, slab)
        return made["two"], qkv_own

    def work_four(sent):
        gate, up = after((made["gate"], made["up"]), sent)
        made["both"] = jnp.concatenate([gate, made["two"][0], up, made["two"][1]], axis=1)
        return made["both"], routed_down

    x_all = ring_gather(
        tokens, {1: work_one, 2: work_two, n_f // 2 - 1: work_three, n_f // 2: work_four}
    )
    both_raw = swap_blocks(after(made["both"], x_all), F)
    g_all = lax.all_gather(after(cotangent, qkv_own), F, axis=0, tiled=True)

    blocks = own + 1
    column = jnp.arange(levels * hidden_own, dtype=jnp.int32)
    block_of = (2 * (column // hidden_own) + at_e % 2) * blocks + jnp.minimum(
        (column % hidden_own) // per_expert, own
    )
    spread = (jnp.arange(n_e * blocks, dtype=jnp.int32)[:, None] == block_of[None, :]).astype(f32)

    x_wide = x_all.astype(f32)
    x_hat = x_wide * inverse_rms(x_wide)
    normed = (x_hat * gain_one).astype(bf16)
    places = jnp.arange(seq, dtype=jnp.int32)
    cosine, sine = rope_tables(places)
    lin = product(normed, w_qkv)
    causal = places[:, None] >= places[None, :]
    saved, mixed_parts = [], []
    for h in range(heads):
        at = h * HEAD_DIM
        q_lin, k_lin, v_lin = [
            lin[:, i * slab + at : i * slab + at + HEAD_DIM] + biases[i, at : at + HEAD_DIM]
            for i in range(3)
        ]
        q = ((q_lin * cosine + swap(q_lin) * sine) * score_scale).astype(bf16)
        k = (k_lin * cosine + swap(k_lin) * sine).astype(bf16)
        v = v_lin.astype(bf16)
        scores = jnp.where(causal, product_t(q, k), -1e30)
        top_score = jnp.max(scores, axis=-1, keepdims=True)
        log_total = top_score + jnp.log(
            jnp.sum(jnp.exp(scores - top_score), axis=-1, keepdims=True)
        )
        probs = jnp.exp(scores - log_total)
        mixed_parts.append(product(probs.astype(bf16), v).astype(bf16))
        saved.append((q, k, v, probs))
    mixed = jnp.concatenate(mixed_parts, axis=1)
    mixed = after(mixed, both_raw)
    mixed_own = swap_blocks(mixed.reshape(n_f, rows, slab), F)
    down_raw = swap_blocks(after(routed_down, mixed_own), F)
    gate_mine = gate_like(both_raw[:, :hidden_own])
    mixed_own = after(mixed_own, gate_mine)
    mixed_own = mixed_own.transpose(1, 0, 2).reshape(rows, width)
    hidden = tokens.astype(f32) + product(mixed_own, w_out)

    ffn_own = (hidden * inverse_rms(hidden) * gain_two).astype(bf16)
    def work_ffn(sent):
        made["up"] = gate_like(after(both_raw, sent)[:, hidden_own:])
        return made["up"]

    w_gate = both_levels(gate_mine)
    ffn_all = ring_gather(ffn_own, {1: work_ffn, n_f // 2 - 1: lambda sent: down_raw})
    w_up = both_levels(made["up"])
    down_mine = jnp.concatenate([full_width(down_raw), shared_wdown.astype(bf16)])
    w_down = both_levels(down_mine)
    ffn_both = jnp.concatenate([ffn_all, sibling(ffn_all)])
    g_both = jnp.concatenate([g_all, sibling(g_all)])

    named = jnp.arange(experts, dtype=jnp.int32).astype(bf16)
    ids = jnp.concatenate([ids_of(at_e), ids_of(at_e ^ 1)])
    selected = jnp.sum((ids[:, :, None] == named).astype(f32), axis=1)
    logits = product_t(ffn_both, route_rows)
    logit_exp = jnp.exp(logits[:, 1:] - jnp.max(logits[:, 1:], axis=-1, keepdims=True))
    route_probs = logit_exp / jnp.sum(logit_exp, axis=-1, keepdims=True)
    shared_scale = jax.nn.sigmoid(logits[:, :1])
    gates = jnp.concatenate(
        [
            (route_probs * selected).reshape(2 * seq, n_e, own),
            jnp.broadcast_to(shared_scale[:, None, :], (2 * seq, n_e, 1)),
        ],
        axis=2,
    ).reshape(2 * seq, n_e * blocks)
    scale = dot(gates, spread, 1, 0, highest)
    pre_gate = product_t(ffn_both, w_gate)
    pre_up = product_t(ffn_both, w_up)
    sig = jax.nn.sigmoid(pre_gate)
    silu = pre_gate * sig
    slope = sig * (1.0 + pre_gate * (1.0 - sig))
    mid = (silu * pre_up).astype(bf16).astype(f32)
    mid_scaled = (mid * scale).astype(bf16)

    def over_levels(grad):
        return lax.psum_scatter(
            grad, E, scatter_dimension=0, tiled=True, axis_index_groups=along_levels
        )

    d_down_all = contract(mid_scaled, g_both).astype(bf16)
    def by_slab(grad):
        return grad.reshape(grad.shape[0], n_f, slab).transpose(1, 0, 2)

    def gate_slabs(grad):
        routed, shared = grad[: own * per_expert], grad[own * per_expert :]
        shared = shared.reshape(per_shared, n_e, n_f, part).transpose(2, 0, 1, 3)
        shared = shared.reshape(n_f, per_shared, slab)
        return jnp.concatenate([by_slab(routed), shared], axis=1)

    def return_routed(back):
        back = back.reshape(n_f, own, per_expert, slab).transpose(1, 0, 2, 3)
        return back.reshape(own, n_f * per_expert, slab)

    def return_gate(back):
        return return_routed(back[:, : own * per_expert]).transpose(0, 2, 1).astype(f32)

    mid_grad = product_t(after(g_both, d_down_all), w_down)
    sums = dot(spread, mid * mid_grad, 1, 1, highest)
    scaled = mid_grad * scale
    gate_grad = (scaled * pre_up * slope).astype(bf16)
    up_grad = (scaled * silu).astype(bf16)

    d_down = over_levels(d_down_all)
    d_gate_all = contract(gate_grad, ffn_both).astype(bf16)
    d_up_all = contract(up_grad, ffn_both).astype(bf16)
    gate_grad, up_grad = lax.optimization_barrier((gate_grad, up_grad, d_gate_all, d_up_all))[:2]

    def input_grad(first):
        rows_of = slice(first, first + seq)
        return product(gate_grad[rows_of], w_gate) + product(up_grad[rows_of], w_up)

    from_sibling = sibling(input_grad(seq).astype(bf16))
    gate_sums = sums[:, :seq] + sibling(sums[:, seq:])
    gate_sums = gate_sums.reshape(n_e * blocks, n_f, rows).transpose(1, 0, 2)
    terms = (input_grad(0) + from_sibling.astype(f32)).astype(bf16)
    gate_sums = jnp.sum(swap_blocks(gate_sums, F), axis=0)
    d_down = after(d_down, terms)
    d_down_back = swap_blocks(after(by_slab(d_down[: own * per_expert]), gate_sums), F)
    d_gate, d_up = over_levels(d_gate_all), over_levels(d_up_all)
    moe_sibling = sibling(product(after(mid_scaled, terms)[seq:], w_down).astype(bf16))
    moe = (product(mid_scaled[:seq], w_down) + moe_sibling.astype(f32)).astype(bf16)
    d_expert_down = return_routed(d_down_back).astype(f32)
    ffn_grad = ring_scatter(
        terms, {3: (gate_sums, moe_sibling), 2: moe, 1: d_expert_down}
    )
    gate_sums = gate_sums.T.reshape(rows, n_e, blocks)

    def mine(table):
        return lax.dynamic_slice_in_dim(table, at_f * rows, rows, 0)

    probs_own, shared_own, selected_own = mine(route_probs), mine(shared_scale), mine(selected)
    prob_grad = gate_sums[:, :, :own].reshape(rows, experts) * selected_own
    logit_grad = probs_own * (
        prob_grad - jnp.sum(probs_own * prob_grad, axis=-1, keepdims=True)
    )
    weight_grad = (
        jnp.sum(gate_sums[:, :, own], axis=1, keepdims=True) * shared_own * (1.0 - shared_own)
    )
    route_grad = jnp.concatenate([weight_grad, logit_grad], axis=1)
    d_route = dot(route_grad, ffn_own.astype(f32), 0, 0, highest)
    ffn_grad = ffn_grad + dot(route_grad, route_rows.astype(f32), 1, 0, highest)
    hidden_back, hidden_hat = norm_back(hidden, gain_two, ffn_grad)
    d_gain_two = jnp.sum(ffn_grad * hidden_hat, axis=0)
    hidden_grad = cotangent.astype(f32) + hidden_back

    hidden_low = hidden_grad.astype(bf16)
    mixed_grad = product_t(hidden_low, w_out).astype(bf16).reshape(rows, n_f, slab)
    mixed_grad = swap_blocks(mixed_grad.transpose(1, 0, 2), F)
    mixed_grad = mixed_grad.reshape(seq, slab)
    hidden_low = lax.all_gather(after(hidden_low, d_up), F, axis=0, tiled=True)
    moe = lax.psum_scatter(after(moe, hidden_low), F, scatter_dimension=0, tiled=True)
    output = (hidden + moe.astype(f32)).astype(bf16)
    lin_grads = [[], [], []]
    for h in range(heads):
        q, k, v, probs = saved[h]
        out_grad = mixed_grad[:, h * HEAD_DIM : (h + 1) * HEAD_DIM]
        p_grad = product_t(out_grad, v)
        delta = jnp.sum(probs * p_grad, axis=-1, keepdims=True)
        s_grad = (probs * (p_grad - delta)).astype(bf16)
        dq = product(s_grad, k) * score_scale
        dk = contract(s_grad, q)
        lin_grads[0].append((dq * cosine - swap(dq) * sine).astype(bf16))
        lin_grads[1].append((dk * cosine - swap(dk) * sine).astype(bf16))
        lin_grads[2].append(contract(probs.astype(bf16), out_grad).astype(bf16))
    lin_grad = jnp.concatenate(lin_grads[0] + lin_grads[1] + lin_grads[2], axis=1)
    normed_part = product_t(lin_grad, w_qkv).astype(bf16)
    gate_back = swap_blocks(after(gate_slabs(d_gate), normed_part), F)
    up_back = swap_blocks(after(gate_slabs(d_up), gate_back), F)
    d_qkv = contract(normed, lin_grad)
    d_expert_gate, d_expert_up = return_gate(gate_back), return_gate(up_back)
    normed_grad = ring_scatter(normed_part, {3: d_qkv})
    d_out = contract(mixed, hidden_low)
    d_bias = jnp.sum(lin_grad.astype(f32), axis=0).reshape(3, slab)
    d_gain_one = jnp.sum(d_qkv * w_qkv.astype(f32), axis=1) / gain_one
    token_back, unused = norm_back(tokens.astype(f32), gain_one, normed_grad)
    token_grad = (hidden_grad + token_back).astype(bf16)

    d_shared_down = d_down[own * per_expert :].astype(f32)
    shared_two = jnp.stack([gate_back[:, own * per_expert :], up_back[:, own * per_expert :]])
    shared_two = shared_two.reshape(2, n_f * per_shared, slab).transpose(0, 2, 1)
    shared_two = shared_two.reshape(2, n_e, part, n_f * per_shared).transpose(1, 0, 2, 3)
    shared_two = swap_blocks(shared_two.reshape(n_e, 2 * part, n_f * per_shared), E)
    shared_two = shared_two.reshape(n_e, 2, part, n_f * per_shared).transpose(1, 2, 0, 3)
    shared_two = shared_two.reshape(2, part, devices * per_shared).astype(f32)

    from_heads = [(e * n_f + f, n_e * f + e) for e in range(n_e) for f in range(n_f)]
    d_out = lax.psum_scatter(d_out.astype(bf16), E, scatter_dimension=0, tiled=True)
    d_wout = lax.ppermute(d_out, EF, from_heads).astype(f32)
    d_qkv = lax.psum_scatter(d_qkv.astype(bf16), E, scatter_dimension=0, tiled=True)
    d_qkv = swap_blocks(d_qkv.reshape(n_f, part, 3 * slab), F)
    d_qkv = d_qkv.reshape(n_f, part, 3, slab).transpose(2, 1, 0, 3).reshape(3, part, width)
    d_qkv = d_qkv.astype(f32)

    bias_rows = lax.dynamic_update_slice_in_dim(
        jnp.zeros((3, width), f32), d_bias, at_f * slab, 1
    )
    d_small = jnp.concatenate([bias_rows, d_gain_one[None], d_gain_two[None], d_route])
    d_small = d_small.reshape(6 + experts, devices, part).transpose(1, 0, 2)
    d_small = jnp.sum(swap_blocks(d_small, EF), axis=0)

    return (
        output,
        token_grad,
        d_qkv[0],
        d_small[0],
        d_qkv[1],
        d_small[1],
        d_qkv[2],
        d_small[2],
        d_wout,
        d_small[3],
        d_small[4],
        d_small[6:].T,
        d_small[5],
        shared_two[0],
        shared_two[1],
        d_shared_down,
        d_expert_gate,
        d_expert_up,
        d_expert_down,
    )


def solution(mesh):
    matrix, vector = P(EF, None), P(EF)
    wide, tall = P(E, F, None), P(E, None, F)
    in_specs = (matrix, matrix) + (matrix, vector) * 3 + (matrix, vector, vector, matrix, vector)
    in_specs = in_specs + (matrix,) * 3 + (wide, wide, tall, matrix)
    out_specs = (matrix, matrix) + (matrix, vector) * 3 + (matrix, vector, vector, matrix, vector)
    out_specs = out_specs + (matrix,) * 3 + (wide, wide, tall)
    return jax.shard_map(shards, mesh=mesh, in_specs=in_specs, out_specs=out_specs, check_vma=False)
```
